32 devices in a mesh: pose: 8 (over z, y), dom: 4 (over x, core).
Axes of the slice: x: 2, y: 2, z: 4, core: 2. Of those that a mesh axis runs over, the one named last changes fastest.
Arguments:
- particles: bfloat16 [4096, 4096], P(('pose', 'dom')), may hold values from -16 to 16
- candidates: int32 [4096, 2], P(('pose', 'dom')), may hold values from 0 to 15, all different within a row; in each aligned block of 128 rows (0 to 127, 128 to 255, ...) at most 48 rows name the same one
- ctf_ids: int32 [4096], P(('pose', 'dom')), may hold values from 0 to 15
- offsets: int32 [4096, 2, 9], P(('pose', 'dom')), may hold values from -3 to 3
- ctf_table: float32 [16, 2048], replicated, may hold values from -1 to 1
- sigma_sq: float32 [2048], replicated, may hold values from 0.5 to 2
- projections: bfloat16 [16, 256, 4096], P('pose', 'dom'), may hold values from -6 to 6
Outputs:
- class_prob: float32 [4096, 2], P(('pose', 'dom'))
- mean_shift: float32 [4096, 2], P(('pose', 'dom'))
The draws below stay inside these ranges and needn't reach their ends.
Inputs may be any that keep to these rules, and one draw needn't show every extreme that they name: `candidates`: each particle names 2 different classes; among the rows of one device no class is named by more than 48 rows, and on some device one class is named by exactly 48.
All inputs are finite; a program needn't handle non-finite values.
Results may differ from the reference program's by a relative error of at most 0.0025.
The reference program's roundings to bfloat16 on the way (of `shifted`) count: a program that leaves them out, or rounds other values in their place, can miss the bound.
Values may be sent and summed in bfloat16 or wider, within the bound.
No kernel may reach another device: no remote copies, remote signals or barrier semaphores. Data moves between devices by JAX's collectives and lax.ppermute only.
A program may use at most 192 MiB of HBM per device.

```python
import math
import jax
import jax.numpy as jnp
import numpy as np
from jax import lax

P_SIZE = 2048
ORI = 256
TRANS = 9
TOP = 2
NCTF = 16
BOX = 128
PART_DEV = 128
CLASSES = 16
NPART = 4096
MOST = 48


def draw_particles(key, part):
    base_key = jax.random.fold_in(key, 21)
    values = jnp.clip(jax.random.normal(base_key, (NPART, 2 * P_SIZE), jnp.float32), -6.0, 6.0)
    return jnp.clip(values, -16.0, 16.0).astype(jnp.bfloat16)


def draw_projections(key, part):
    noise = jnp.clip(jax.random.normal(jax.random.fold_in(key, 31), (CLASSES, ORI, 2 * P_SIZE), jnp.float32), -6.0, 6.0)
    values = noise
    return jnp.clip(values, -6.0, 6.0).astype(jnp.bfloat16)


def draw_ctf_table(key, part):
    values = jax.random.uniform(jax.random.fold_in(key, 41), (NCTF, P_SIZE), jnp.float32, -1.0, 1.0)
    return values


def with_ends(array, rng, smallest, largest):
    longest = array.shape.index(max(array.shape))
    spots = []
    for shift in (0, 1):
        where = [jax.random.randint(jax.random.fold_in(rng, axis), (), 0, length) for axis, length in enumerate(array.shape)]
        where[longest] = (where[longest] + shift) % array.shape[longest]
        spots.append(tuple(where))
    return array.at[spots[0]].set(smallest).at[spots[1]].set(largest)


def assign_block(rng, own, number, rows, count, top, reach, skew):
    sequence = jax.random.permutation(rng, count)
    heavy_load, common = portions_of(count, rows * top, reach, skew, True), portions_of(count, rows * top, reach, skew, False)
    places = jnp.arange(count)

    def named(tallies, rotation):
        used = int((tallies > 0).sum())
        fixed = max(1, used // 4)
        moved = fixed + (places - fixed + rotation * (used - fixed)) % max(1, count - fixed)
        return jnp.zeros((count,), jnp.int32).at[sequence[jnp.where(places < fixed, places, moved)]].set(jnp.asarray(tallies, jnp.int32))

    tallies = jnp.where(number % 4 == 0, named(heavy_load, number // 4), named(common, number - number // 4 - 1))
    mixed = jax.random.permutation(jax.random.fold_in(own, 3), count)
    donor, receiver = mixed[0:count // 2 * 2:2], mixed[1:count // 2 * 2:2]
    slack = jnp.minimum(tallies[donor] - 1, reach - tallies[receiver]) // 2
    slack = jnp.where((donor == sequence[0]) | (receiver == sequence[0]) | (tallies[receiver] == 0), 0, jnp.maximum(slack, 0))
    moved = jax.random.randint(jax.random.fold_in(own, 4), (count // 2,), 0, 1 << 20) % (slack + 1)
    tallies = tallies.at[donor].add(-moved).at[receiver].add(moved)
    items = jnp.searchsorted(jnp.cumsum(tallies), jnp.arange(rows * top), side="right").astype(jnp.int32)
    table = items.reshape(top, rows).T
    table = table[jax.random.permutation(jax.random.fold_in(own, 1), rows)]
    rotation = jax.random.randint(jax.random.fold_in(own, 2), (rows, 1), 0, top)
    return jnp.take_along_axis(table, (jnp.arange(top)[None, :] + rotation) % top, axis=1)


def portions_of(number_of, total, limit, skew, full):
    loads = [(1 << 20) // math.isqrt(grade ** skew) + 1 for grade in range(1, number_of + 1)]
    largest = limit if full else min(limit, max(-(-total // number_of), total * loads[0] // sum(loads)))
    least = 1 if total - largest >= number_of - 1 else 0
    holding, surplus = [largest] + [least] * (number_of - 1), total - largest - least * (number_of - 1)
    while surplus > 0:
        free = [i for i in range(1, number_of) if holding[i] < largest] or [i for i in range(1, number_of) if holding[i] < limit]
        pool, budget = sum([loads[i] for i in free]), surplus
        for i in free:
            addition = min(limit - holding[i], max(1, budget * loads[i] // pool), surplus)
            holding[i] = holding[i] + addition
            surplus = surplus - addition
    return np.array(holding)


def setup_inputs(seed: int = 0) -> dict:
    seeds = jax.random.split(jax.random.key(seed), 8)
    particles = draw_particles(jax.random.fold_in(seeds[7], 71), 0)
    candidates_keys = jax.random.split(jax.random.fold_in(seeds[1], 1), NPART // PART_DEV)
    candidates_turns = jax.random.permutation(jax.random.fold_in(seeds[1], 3), NPART // PART_DEV)
    candidates = jax.vmap(lambda own, number: assign_block(jax.random.fold_in(seeds[1], 2), own, number, PART_DEV, CLASSES, TOP, MOST, 2))(candidates_keys, candidates_turns).reshape((NPART, TOP))
    ctf_ids = with_ends(jax.random.randint(seeds[2], (NPART,), 0, NCTF), jax.random.fold_in(seeds[2], 1), 0, NCTF - 1).astype(jnp.int32)
    offsets = with_ends(jax.random.randint(seeds[3], (NPART, 2, TRANS), -3, 4), jax.random.fold_in(seeds[3], 1), -3, 3).astype(jnp.int32)
    ctf_table = draw_ctf_table(jax.random.fold_in(seeds[7], 71), 0)
    sigma_sq = jnp.clip(jnp.exp(jax.random.uniform(seeds[5], (P_SIZE,), jnp.float32, math.log(0.5), math.log(2.0))), 0.5, 2.0)
    projections = draw_projections(jax.random.fold_in(seeds[7], 71), 0)
    return {"particles": particles, "candidates": candidates, "ctf_ids": ctf_ids, "offsets": offsets, "ctf_table": ctf_table, "sigma_sq": sigma_sq, "projections": projections}


two_pi = 6.283185307179586


def reference(particles, candidates, ctf_ids, offsets, ctf_table, sigma_sq, projections):
    stacked = projections.astype(jnp.float32)
    power_rows = stacked[:, :, :P_SIZE] ** 2 + stacked[:, :, P_SIZE:] ** 2
    pixel_index = jnp.arange(P_SIZE, dtype=jnp.int32)
    freq_x = ((pixel_index % 64) - 32).astype(jnp.float32) * (two_pi / BOX)
    freq_y = (pixel_index // 64).astype(jnp.float32) * (two_pi / BOX)
    block_rows = 32

    def one_block(block_index):
        first_row = (block_index * block_rows).astype(jnp.int32)
        particle_rows = lax.dynamic_slice_in_dim(particles, first_row, block_rows, 0).astype(jnp.float32)
        chosen = lax.dynamic_slice_in_dim(candidates, first_row, block_rows, 0)
        shifts = lax.dynamic_slice_in_dim(offsets, first_row, block_rows, 0).astype(jnp.float32)
        ctf_index = lax.dynamic_slice_in_dim(ctf_ids, first_row, block_rows, 0)
        ctf_rows = ctf_table[ctf_index]
        weight = ctf_rows / sigma_sq[None, :]
        damping = weight * ctf_rows
        phase_angle = shifts[:, 0, :, None] * freq_x + shifts[:, 1, :, None] * freq_y
        cosine = jnp.cos(phase_angle)
        sine_part = jnp.sin(phase_angle)
        real_part = particle_rows[:, None, :P_SIZE]
        imag_part = particle_rows[:, None, P_SIZE:]
        shifted = jnp.concatenate([weight[:, None, :] * (real_part * cosine + imag_part * sine_part),
                                   weight[:, None, :] * (imag_part * cosine - real_part * sine_part)], axis=2)
        shifted = lax.optimization_barrier(shifted.astype(jnp.bfloat16)).astype(jnp.float32)
        weights_log = []
        totals = []
        moments_x = []
        moments_y = []
        for column in range(TOP):
            class_col = chosen[:, column]
            class_views = stacked[class_col]
            class_power = power_rows[class_col]
            scores = jnp.einsum('btk,bok->bto', shifted, class_views, precision=lax.Precision.HIGHEST)
            penalty = -0.5 * jnp.einsum('bp,bop->bo', damping, class_power, precision=lax.Precision.HIGHEST)
            scores = scores + penalty[:, None, :]
            highest = jnp.max(scores, axis=(1, 2))
            exp_terms = jnp.exp(scores - highest[:, None, None])
            per_shift = jnp.sum(exp_terms, axis=2)
            total = jnp.sum(per_shift, axis=1)
            weights_log.append(highest + jnp.log(total))
            totals.append(total)
            moments_x.append(jnp.sum(per_shift * shifts[:, 0, :], axis=1))
            moments_y.append(jnp.sum(per_shift * shifts[:, 1, :], axis=1))
        log_weight = jnp.stack(weights_log, axis=1)
        total_all = jnp.stack(totals, axis=1)
        highest_log = jnp.max(log_weight, axis=1, keepdims=True)
        raw_weight = jnp.exp(log_weight - highest_log)
        class_prob = raw_weight / jnp.sum(raw_weight, axis=1, keepdims=True)
        mean_x = jnp.sum(class_prob * jnp.stack(moments_x, axis=1) / total_all, axis=1)
        mean_y = jnp.sum(class_prob * jnp.stack(moments_y, axis=1) / total_all, axis=1)
        return class_prob, jnp.stack([mean_x, mean_y], axis=1)

    prob_blocks, mean_blocks = lax.map(one_block, jnp.arange(NPART // block_rows, dtype=jnp.int32))
    return prob_blocks.reshape(NPART, TOP), mean_blocks.reshape(NPART, 2)
```

```python
import functools

import jax
import jax.numpy as jnp
import ml_dtypes
import numpy as np
from jax import lax
from jax.experimental import pallas as pl
from jax.experimental.pallas import tpu as pltpu
from jax.sharding import PartitionSpec as P

BOX = 128
GRID_X = 64
REACH = 3
SHARE = 4
TILE = 32
CHUNK = 256
HIGHEST = lax.Precision.HIGHEST


def split_three(values):
    parts = []
    for _ in range(3):
        part = lax.reduce_precision(values, 8, 7)
        parts.append(part.astype(jnp.bfloat16))
        values = values - part
    return parts


def phase_table(pixel_count):
    levels = np.arange(-REACH, REACH + 1)
    pixel = np.arange(pixel_count)
    shift_x = np.repeat(levels, levels.size)[:, None]
    shift_y = np.tile(levels, levels.size)[:, None]
    angle = 2.0 * np.pi / BOX * (shift_x * (pixel % GRID_X - 32) + shift_y * (pixel // GRID_X))
    rest = np.concatenate([np.cos(angle), np.sin(angle)], axis=1).astype(np.float32)
    parts = []
    for _ in range(3):
        part = rest.astype(ml_dtypes.bfloat16)
        parts.append(part)
        rest = rest - part.astype(np.float32)
    rows = np.concatenate(parts, axis=0)
    count = levels.size**2
    padded = np.zeros((256, 2 * pixel_count), ml_dtypes.bfloat16)
    padded[: rows.shape[0]] = rows
    label = np.full((1, 256), -1.0, np.float32)
    label[0, : rows.shape[0]] = np.arange(rows.shape[0]) % count
    return (padded, label)


def swap(values, axis, bit):
    count = lax.axis_size(axis)
    return lax.ppermute(values, axis, [(index, index ^ bit) for index in range(count)])


def stats_kernel(share, pieces, trans, tiles_ref, rank_ref, meta_ref, label_ref, table_ref, wtab_ref,
                 pen_ref, *refs):
    x_refs = refs[:share]
    q_refs = refs[share:share + pieces]
    out_ref, parts, proj, uv, pens, info, stats = refs[share + pieces:]
    step = pl.program_id(0)
    rows_x = x_refs[0].shape[0]
    rows_q = q_refs[0].shape[1]
    slots = uv.shape[0]
    pixels = uv.shape[1] // 2
    rows_all = parts.shape[0]

    @pl.when(step == 0)
    def _():
        for index in range(share):
            parts[index * rows_x:(index + 1) * rows_x, :] = x_refs[index][...]

    for index in range(pieces):
        proj[index * rows_q:(index + 1) * rows_q, :] = q_refs[index][0]

    chosen = rank_ref[0] == lax.broadcasted_iota(jnp.int32, (slots, rows_all), 0)
    pick = jnp.where(chosen, 1.0, 0.0).astype(jnp.bfloat16)
    info[...] = jnp.dot(pick, meta_ref[...], preferred_element_type=jnp.float32)
    group = info[:, trans:trans + 1]
    lane = lax.broadcasted_iota(jnp.int32, (slots, 128), 1)
    group_hot = jnp.where(group == (lane % 16).astype(jnp.float32), 1.0, 0.0)
    group_bf = jnp.where(lane < 48, group_hot, 0.0).astype(jnp.bfloat16)
    pens[...] = jnp.dot(group_hot[:, :16], pen_ref[0], precision=HIGHEST,
                        preferred_element_type=jnp.float32)
    for first in range(0, pixels, CHUNK):
        cols = slice(first, first + CHUNK)
        icols = slice(pixels + first, pixels + first + CHUNK)
        weight = jnp.dot(group_bf, wtab_ref[:, cols], preferred_element_type=jnp.float32)
        uv[:, cols] = weight * jnp.dot(pick, parts[:, cols], preferred_element_type=jnp.float32)
        uv[:, icols] = weight * jnp.dot(pick, parts[:, icols], preferred_element_type=jnp.float32)
    stats[...] = jnp.zeros_like(stats)
    label = label_ref[...]

    @pl.loop(0, tiles_ref[step])
    def _(tile):
        rows = pl.ds(pl.multiple_of(tile * TILE, TILE), TILE)
        here = info[rows, :]
        hot = jnp.concatenate(
            [jnp.where(here[:, t:t + 1] == label, 1.0, 0.0) for t in range(trans)], axis=0
        ).astype(jnp.bfloat16)
        scores = jnp.zeros((trans * TILE, proj.shape[0]), jnp.float32)
        for first in range(0, pixels, CHUNK):
            cols = slice(first, first + CHUNK)
            icols = slice(pixels + first, pixels + first + CHUNK)
            cosine = jnp.dot(hot, table_ref[:, cols], preferred_element_type=jnp.float32)
            sine = jnp.dot(hot, table_ref[:, icols], preferred_element_type=jnp.float32)
            cosine = cosine.reshape(trans, TILE, CHUNK)
            sine = sine.reshape(trans, TILE, CHUNK)
            real = uv[rows, cols][None]
            imag = uv[rows, icols][None]
            shift_re = (real * cosine + imag * sine).astype(jnp.bfloat16)
            shift_im = (imag * cosine - real * sine).astype(jnp.bfloat16)
            contract = (((1,), (1,)), ((), ()))
            scores += lax.dot_general(shift_re.reshape(trans * TILE, CHUNK), proj[:, cols], contract,
                                      preferred_element_type=jnp.float32)
            scores += lax.dot_general(shift_im.reshape(trans * TILE, CHUNK), proj[:, icols], contract,
                                      preferred_element_type=jnp.float32)
        full = scores.reshape(trans, TILE, proj.shape[0]) + pens[rows, :][None]
        highest = jnp.max(jnp.max(full, axis=0), axis=1, keepdims=True)
        total = jnp.zeros((TILE, proj.shape[0]), jnp.float32)
        moment_x = jnp.zeros((TILE, proj.shape[0]), jnp.float32)
        moment_y = jnp.zeros((TILE, proj.shape[0]), jnp.float32)
        for t in range(trans):
            term = jnp.exp(full[t] - highest)
            total += term
            moment_x += term * here[:, trans + 1 + t:trans + 2 + t]
            moment_y += term * here[:, 2 * trans + 1 + t:2 * trans + 2 + t]
        total = jnp.sum(total, axis=1, keepdims=True)
        moment_x = jnp.sum(moment_x, axis=1, keepdims=True)
        moment_y = jnp.sum(moment_y, axis=1, keepdims=True)
        lanes = lax.broadcasted_iota(jnp.int32, (TILE, 128), 1)
        stats[rows, :] = jnp.where(
            lanes == 0, highest,
            jnp.where(lanes == 1, total, jnp.where(lanes == 2, moment_x,
                                                   jnp.where(lanes == 3, moment_y, 0.0))))

    back = lax.dot_general(stats[...], jnp.where(chosen, 1.0, 0.0), (((0,), (0,)), ((), ())),
                           precision=HIGHEST, preferred_element_type=jnp.float32)
    out_ref[0] = back[:8, :]


def class_stats(tiles, rank, meta, label, table, wtab, pen, x_parts, q_parts, trans, slots):
    classes, _, rows_all = rank.shape
    share, pieces = len(x_parts), len(q_parts)
    rows_q, width = q_parts[0].shape[1:]
    whole = lambda array: pl.BlockSpec(array.shape, lambda c, tiles: (0,) * array.ndim)
    per_class = lambda array: pl.BlockSpec((1,) + array.shape[1:], lambda c, tiles: (c, 0, 0))
    ori = rows_q * pieces
    return pl.pallas_call(
        functools.partial(stats_kernel, share, pieces, trans),
        out_shape=jax.ShapeDtypeStruct((classes, 8, rows_all), jnp.float32),
        grid_spec=pltpu.PrefetchScalarGridSpec(
            num_scalar_prefetch=1,
            grid=(classes,),
            in_specs=[per_class(rank), whole(meta), whole(label), whole(table), whole(wtab), per_class(pen)]
            + [whole(array) for array in x_parts]
            + [per_class(array) for array in q_parts],
            out_specs=pl.BlockSpec((1, 8, rows_all), lambda c, tiles: (c, 0, 0)),
            scratch_shapes=[
                pltpu.VMEM((rows_all, width), jnp.bfloat16),
                pltpu.VMEM((ori, width), jnp.bfloat16),
                pltpu.VMEM((slots, width), jnp.float32),
                pltpu.VMEM((slots, ori), jnp.float32),
                pltpu.VMEM((slots, 128), jnp.float32),
                pltpu.VMEM((slots, 128), jnp.float32),
            ],
        ),
        compiler_params=pltpu.CompilerParams(vmem_limit_bytes=56 * 1024 * 1024),
        cost_estimate=pl.CostEstimate(
            flops=classes * slots * trans * width * (ori + 256),
            bytes_accessed=(rows_all + classes * ori) * width * 2,
            transcendentals=0,
        ),
    )(tiles, rank, meta, label, table, wtab, pen, *x_parts, *q_parts)


def on_device(particles, candidates, ctf_ids, offsets, ctf_table, sigma_sq, projections):
    pose_count = lax.axis_size("pose")
    dom_count = lax.axis_size("dom")
    pose = lax.axis_index("pose")
    local = projections.shape[0]
    class_total = local * pose_count
    rows, picks = candidates.shape
    trans = offsets.shape[2]
    pixels = sigma_sq.shape[0]
    capacity = 3 * rows * picks // class_total
    share = min(SHARE, pose_count)
    share_bits = [1 << b for b in range(share.bit_length() - 1)]
    class_bits = [share << b for b in range((pose_count // share).bit_length() - 1)]
    dom_bits = [1 << b for b in range(dom_count.bit_length() - 1)][::-1]
    slots = -(-min(share * capacity, share * rows) // TILE) * TILE

    offset_f = offsets.astype(jnp.float32)
    combo = (offset_f[:, 0] + REACH) * (2 * REACH + 1) + (offset_f[:, 1] + REACH)
    meta = jnp.concatenate(
        [combo, ctf_ids[:, None].astype(jnp.float32), offset_f[:, 0], offset_f[:, 1],
         candidates.astype(jnp.float32)], axis=1)
    meta = jnp.pad(meta, ((0, 0), (0, 128 - meta.shape[1]))).astype(jnp.bfloat16)
    families = [projections]
    for bit in class_bits:
        families += [swap(member, "pose", bit) for member in families]
    x_parts, metas = [particles], meta[None]
    for bit in share_bits[::-1]:
        x_parts = x_parts + [swap(member, "pose", bit) for member in x_parts]
        metas = jnp.concatenate([metas, swap(metas, "pose", bit)], axis=0)
    order = [0]
    for bit in share_bits[::-1]:
        order = order + [member ^ bit for member in order]

    weight = ctf_table / sigma_sq[None, :]
    wide = projections.astype(jnp.float32)
    power = wide[:, :, :pixels] ** 2 + wide[:, :, pixels:] ** 2
    pen = -0.5 * jnp.einsum("gp,cop->cgo", weight * ctf_table, power, precision=HIGHEST)
    pens = pen[None]
    for bit in class_bits:
        pens = jnp.concatenate([pens, swap(pens, "pose", bit)], axis=0)
    for bit in dom_bits:
        pens = jnp.concatenate([pens, swap(pens, "dom", bit)], axis=3)
    group_count = ctf_table.shape[0]
    wtab = jnp.pad(jnp.concatenate(split_three(weight), axis=0), ((0, 128 - 3 * group_count), (0, 0)))

    meta_all = metas.reshape(share * rows, 128)
    named = meta_all[:, 3 * trans + 1:3 * trans + 1 + picks].astype(jnp.int32)
    family_count = len(families)
    owner = pose ^ (jnp.arange(family_count, dtype=jnp.int32) * share)
    class_ids = (owner[:, None] * local + jnp.arange(local, dtype=jnp.int32)[None, :]).reshape(-1)
    names = jnp.any(named.T[None, :, :] == class_ids[:, None, None], axis=1).astype(jnp.int32)
    ahead = jnp.cumsum(names, axis=1)
    rank = jnp.where(names > 0, ahead - 1, -1)[:, None, :]
    tiles = (ahead[:, -1] + (TILE - 1)) // TILE

    table, label = phase_table(pixels)
    table, label = jnp.asarray(table), jnp.asarray(label)
    results = []
    for index in range(family_count):
        q_parts = [families[index]]
        for bit in dom_bits:
            q_parts = q_parts + [swap(member, "dom", bit) for member in q_parts]
        span = slice(index * local, (index + 1) * local)
        results.append(class_stats(tiles[span], rank[span], meta_all, label, table, wtab, pens[index],
                                   x_parts, q_parts, trans, slots))
    stats = jnp.concatenate(results, axis=0)[:, :4, :]

    own = []
    for place, member in enumerate(order):
        block = stats[:, :, place * rows:(place + 1) * rows]
        own.append((member, swap(block, "pose", member) if member else block))
    cand = candidates.T
    owner = cand // local
    beyond = (owner ^ pose) // share
    within = (owner ^ pose) % share
    position = beyond * local + cand % local
    picked = jnp.zeros((picks, 4, rows), jnp.float32)
    for member, block in own:
        for spot in range(family_count * local):
            hit = (within == member) & (position == spot)
            picked = jnp.where(hit[:, None, :], block[spot][None], picked)
    log_weight = picked[:, 0] + jnp.log(picked[:, 1])
    raw_weight = jnp.exp(log_weight - jnp.max(log_weight, axis=0, keepdims=True))
    class_prob = raw_weight / jnp.sum(raw_weight, axis=0, keepdims=True)
    mean_x = jnp.sum(class_prob * picked[:, 2] / picked[:, 1], axis=0)
    mean_y = jnp.sum(class_prob * picked[:, 3] / picked[:, 1], axis=0)
    return (class_prob.T, jnp.stack([mean_x, mean_y], axis=1))


def solution(mesh):
    in_specs = (
        P(("pose", "dom"), None),
        P(("pose", "dom"), None),
        P(("pose", "dom")),
        P(("pose", "dom"), None, None),
        P(),
        P(),
        P("pose", "dom", None),
    )
    out_specs = (P(("pose", "dom"), None), P(("pose", "dom"), None))
    return jax.shard_map(
        on_device, mesh=mesh, in_specs=in_specs, out_specs=out_specs, check_vma=False
    )
```

```python
import functools

import jax
import jax.numpy as jnp
import ml_dtypes
import numpy as np
from jax import lax
from jax.experimental import pallas as pl
from jax.experimental.pallas import tpu as pltpu
from jax.sharding import PartitionSpec as P

BOX = 128
GRID_X = 64
REACH = 3
SHARE = 4
TILE = 32
CHUNK = 512
BLOCK = 256
HIGHEST = lax.Precision.HIGHEST


def split_three(values):
    parts = []
    for _ in range(3):
        part = lax.reduce_precision(values, 8, 7)
        parts.append(part.astype(jnp.bfloat16))
        values = values - part
    return parts


def phase_table(pixel_count):
    levels = np.arange(-REACH, REACH + 1)
    pixel = np.arange(pixel_count)
    shift_x = np.repeat(levels, levels.size)[:, None]
    shift_y = np.tile(levels, levels.size)[:, None]
    angle = 2.0 * np.pi / BOX * (shift_x * (pixel % GRID_X - 32) + shift_y * (pixel // GRID_X))
    rest = np.concatenate([np.cos(angle), np.sin(angle)], axis=1).astype(np.float32)
    parts = []
    for _ in range(3):
        part = rest.astype(ml_dtypes.bfloat16)
        parts.append(part)
        rest = rest - part.astype(np.float32)
    rows = np.concatenate(parts, axis=0)
    count = levels.size**2
    padded = np.zeros((256, 2 * pixel_count), ml_dtypes.bfloat16)
    padded[: rows.shape[0]] = rows
    padded = padded.reshape(256, 2, pixel_count // CHUNK, CHUNK).transpose(0, 2, 1, 3).reshape(256, -1)
    label = np.full((1, 256), -1.0, np.float32)
    label[0, : rows.shape[0]] = np.arange(rows.shape[0]) % count
    return (padded, label)


def swap(values, axis, bit):
    count = lax.axis_size(axis)
    return lax.ppermute(values, axis, [(index, index ^ bit) for index in range(count)])


def stats_kernel(share, pieces, classes, trans, tiles_ref, rank_ref, meta_ref, label_ref, table_ref,
                 wtab_ref, pen_ref, *refs):
    x_refs = refs[:share]
    q_refs = refs[share:share + pieces * classes]
    out_ref, parts, proj, uv, pens, info, stats = refs[share + pieces * classes:]
    step = pl.program_id(0)
    rows_x = x_refs[0].shape[0]
    slots = uv.shape[0]
    pixels = uv.shape[1] // 2
    rows_all = parts.shape[0]
    ori = proj.shape[1]

    @pl.when(step == 0)
    def _():
        for index in range(share):
            parts[index * rows_x:(index + 1) * rows_x, :] = x_refs[index][...]

    def source(first):
        chunk, inside = divmod(first, 2 * CHUNK)
        return chunk * CHUNK + inside % CHUNK + (pixels if inside >= CHUNK else 0)

    for place in range(classes):
        @pl.when(step == place)
        def _():
            members = q_refs[place * pieces:(place + 1) * pieces]
            for first in range(0, 2 * pixels, BLOCK):
                cols = slice(source(first), source(first) + BLOCK)
                block = jnp.concatenate([member[0, :, cols] for member in members], axis=0)
                proj[first:first + BLOCK, :] = block.T

    chosen = rank_ref[0] == lax.broadcasted_iota(jnp.int32, (slots, rows_all), 0)
    pick = jnp.where(chosen, 1.0, 0.0).astype(jnp.bfloat16)
    info[...] = jnp.dot(pick, meta_ref[...], preferred_element_type=jnp.float32)
    group = info[:, trans:trans + 1]
    groups = pen_ref.shape[1]
    lane = lax.broadcasted_iota(jnp.int32, (slots, 128), 1)
    group_hot = jnp.where(group == (lane % groups).astype(jnp.float32), 1.0, 0.0)
    group_bf = jnp.where(lane < 3 * groups, group_hot, 0.0).astype(jnp.bfloat16)
    pens[...] = jnp.dot(group_hot[:, :groups], pen_ref[0], precision=HIGHEST,
                        preferred_element_type=jnp.float32)
    for first in range(0, pixels, CHUNK):
        weight = jnp.dot(group_bf, wtab_ref[:, first:first + CHUNK], preferred_element_type=jnp.float32)
        for part in range(2):
            start = part * pixels + first
            rows = jnp.dot(pick, parts[:, start:start + CHUNK], preferred_element_type=jnp.float32)
            place = 2 * first + part * CHUNK
            uv[:, place:place + CHUNK] = weight * rows
    stats[...] = jnp.zeros_like(stats)
    label = label_ref[...]

    def one_tile(start, size):
        rows = pl.ds(pl.multiple_of(start, TILE), size)
        here = info[rows, :]
        hot = jnp.concatenate(
            [jnp.where(here[:, t:t + 1] == label, 1.0, 0.0) for t in range(trans)], axis=0
        ).astype(jnp.bfloat16)
        scores = jnp.zeros((trans * size, ori), jnp.float32)
        for first in range(0, 2 * pixels, 2 * CHUNK):
            phase = jnp.dot(hot, table_ref[:, first:first + 2 * CHUNK], preferred_element_type=jnp.float32)
            cosine = phase[:, :CHUNK].reshape(trans, size, CHUNK)
            sine = phase[:, CHUNK:].reshape(trans, size, CHUNK)
            real = uv[rows, first:first + CHUNK][None]
            imag = uv[rows, first + CHUNK:first + 2 * CHUNK][None]
            shifted = jnp.concatenate(
                [(real * cosine + imag * sine).astype(jnp.bfloat16).reshape(trans * size, CHUNK),
                 (imag * cosine - real * sine).astype(jnp.bfloat16).reshape(trans * size, CHUNK)], axis=1)
            scores += jnp.dot(shifted, proj[first:first + 2 * CHUNK, :], preferred_element_type=jnp.float32)
        full = scores.reshape(trans, size, ori) + pens[rows, :][None]
        highest = jnp.max(jnp.max(full, axis=0), axis=1, keepdims=True)
        total = jnp.zeros((size, ori), jnp.float32)
        moment_x = jnp.zeros((size, ori), jnp.float32)
        moment_y = jnp.zeros((size, ori), jnp.float32)
        for t in range(trans):
            term = jnp.exp(full[t] - highest)
            total += term
            moment_x += term * here[:, trans + 1 + t:trans + 2 + t]
            moment_y += term * here[:, 2 * trans + 1 + t:2 * trans + 2 + t]
        total = jnp.sum(total, axis=1, keepdims=True)
        moment_x = jnp.sum(moment_x, axis=1, keepdims=True)
        moment_y = jnp.sum(moment_y, axis=1, keepdims=True)
        lanes = lax.broadcasted_iota(jnp.int32, (size, 128), 1)
        stats[rows, :] = jnp.where(
            lanes == 0, highest,
            jnp.where(lanes == 1, total, jnp.where(lanes == 2, moment_x,
                                                   jnp.where(lanes == 3, moment_y, 0.0))))

    tiles = tiles_ref[step]

    @pl.loop(0, tiles // 2)
    def _(pair):
        one_tile(pair * (2 * TILE), 2 * TILE)

    @pl.when(tiles % 2 == 1)
    def _():
        one_tile((tiles - 1) * TILE, TILE)

    back = lax.dot_general(stats[...], jnp.where(chosen, 1.0, 0.0), (((0,), (0,)), ((), ())),
                           precision=HIGHEST, preferred_element_type=jnp.float32)
    out_ref[0] = back[:8, :]


def class_stats(tiles, rank, meta, label, table, wtab, pen, x_parts, q_parts, trans, slots):
    classes, _, rows_all = rank.shape
    share, pieces = len(x_parts), len(q_parts[0])
    rows_q, width = q_parts[0][0][0].shape[1:]
    whole = lambda array: pl.BlockSpec(array.shape, lambda c, tiles: (0,) * array.ndim)
    per_class = lambda array: pl.BlockSpec((1,) + array.shape[1:], lambda c, tiles: (c, 0, 0))

    def piece_spec(array, spot):
        return pl.BlockSpec((1,) + array.shape[1:], lambda c, tiles: (spot, 0, 0))

    ori = rows_q * pieces
    flat = [piece for members in q_parts for piece in members]
    return pl.pallas_call(
        functools.partial(stats_kernel, share, pieces, classes, trans),
        out_shape=jax.ShapeDtypeStruct((classes, 8, rows_all), jnp.float32),
        grid_spec=pltpu.PrefetchScalarGridSpec(
            num_scalar_prefetch=1,
            grid=(classes,),
            in_specs=[per_class(rank), whole(meta), whole(label), whole(table), whole(wtab), per_class(pen)]
            + [whole(array) for array in x_parts]
            + [piece_spec(array, spot) for array, spot in flat],
            out_specs=pl.BlockSpec((1, 8, rows_all), lambda c, tiles: (c, 0, 0)),
            scratch_shapes=[
                pltpu.VMEM((rows_all, width), jnp.bfloat16),
                pltpu.VMEM((width, ori), jnp.bfloat16),
                pltpu.VMEM((slots, width), jnp.float32),
                pltpu.VMEM((slots, ori), jnp.float32),
                pltpu.VMEM((slots, 128), jnp.float32),
                pltpu.VMEM((slots, 128), jnp.float32),
            ],
        ),
        compiler_params=pltpu.CompilerParams(vmem_limit_bytes=56 * 1024 * 1024),
        cost_estimate=pl.CostEstimate(
            flops=classes * slots * trans * width * (ori + 256),
            bytes_accessed=(rows_all + classes * ori) * width * 2,
            transcendentals=0,
        ),
    )(tiles, rank, meta, label, table, wtab, pen, *x_parts, *[array for array, _ in flat])


def on_device(particles, candidates, ctf_ids, offsets, ctf_table, sigma_sq, projections):
    pose_count = lax.axis_size("pose")
    dom_count = lax.axis_size("dom")
    pose = lax.axis_index("pose")
    local = projections.shape[0]
    class_total = local * pose_count
    rows, picks = candidates.shape
    trans = offsets.shape[2]
    pixels = sigma_sq.shape[0]
    capacity = 3 * rows * picks // class_total
    share = min(SHARE, pose_count)
    families = pose_count // share
    slots = -(-min(share * capacity, share * rows) // TILE) * TILE

    low_groups = [[base + low for low in range(share)] for base in range(0, pose_count, share)]
    everyone = lax.all_gather(particles, "pose", axis_index_groups=low_groups, tiled=True)

    dom_bits = [1 << b for b in range(dom_count.bit_length() - 1)][::-1]
    dom_order = [0]
    for bit in dom_bits:
        dom_order = dom_order + [member ^ bit for member in dom_order]

    def over_dom(array):
        members = [array]
        for bit in dom_bits:
            members = members + [swap(member, "dom", bit) for member in members]
        return members

    q_parts = []
    own_pieces = over_dom(projections)
    q_parts.append([[(piece, spot) for piece in own_pieces] for spot in range(local)])
    for family in range(1, families):
        members = []
        for spot in range(local):
            pieces = over_dom(swap(projections[spot:spot + 1], "pose", family * share))
            members.append([(piece, 0) for piece in pieces])
        q_parts.append(members)

    early = own_pieces[-2] if dom_count > 1 else projections
    offsets, own_view, _ = lax.optimization_barrier((offsets, projections, early))
    offset_f = offsets.astype(jnp.float32)
    combo = (offset_f[:, 0] + REACH) * (2 * REACH + 1) + (offset_f[:, 1] + REACH)
    meta = jnp.concatenate(
        [combo, ctf_ids[:, None].astype(jnp.float32), offset_f[:, 0], offset_f[:, 1],
         candidates.astype(jnp.float32)], axis=1)
    meta = jnp.pad(meta, ((0, 0), (0, 128 - meta.shape[1]))).astype(jnp.bfloat16)
    meta_all = lax.all_gather(meta, "pose", axis_index_groups=low_groups, tiled=True)

    weight = ctf_table / sigma_sq[None, :]
    wide = own_view.astype(jnp.float32)
    power = wide[:, :, :pixels] ** 2 + wide[:, :, pixels:] ** 2
    pen = -0.5 * jnp.einsum("gp,cop->cgo", weight * ctf_table, power, precision=HIGHEST)
    high_groups = [list(range(low, pose_count, share)) for low in range(share)]
    pens = lax.all_gather(lax.all_gather(pen, "dom"), "pose", axis_index_groups=high_groups)
    pens = jnp.take(pens, (pose // share) ^ jnp.arange(families), axis=0)
    pens = jnp.take(pens, lax.axis_index("dom") ^ jnp.array(dom_order), axis=1)
    pens = pens.transpose(0, 2, 3, 1, 4).reshape(families, local, pen.shape[1], -1)
    wtab = jnp.concatenate(split_three(weight), axis=0)
    wtab = jnp.pad(wtab, ((0, 128 - wtab.shape[0]), (0, 0)))

    named = meta_all[:, 3 * trans + 1:3 * trans + 1 + picks].astype(jnp.int32)
    owner = pose ^ (jnp.arange(families, dtype=jnp.int32) * share)
    class_ids = (owner[:, None] * local + jnp.arange(local, dtype=jnp.int32)[None, :]).reshape(-1)
    names = jnp.any(named.T[None, :, :] == class_ids[:, None, None], axis=1).astype(jnp.int32)
    ahead = jnp.cumsum(names, axis=1)
    rank = jnp.where(names > 0, ahead - 1, -1)[:, None, :]
    tiles = (ahead[:, -1] + (TILE - 1)) // TILE

    table, label = phase_table(pixels)
    table, label = jnp.asarray(table), jnp.asarray(label)
    results = []
    for family in range(families):
        spans = [(0, local)] if family == 0 else [(spot, spot + 1) for spot in range(local)]
        for first, last in spans:
            span = slice(family * local + first, family * local + last)
            if results:
                tiles, results[-1] = lax.optimization_barrier((tiles, results[-1]))
            results.append(
                class_stats(tiles[span], rank[span], meta_all, label, table, wtab, pens[family][first:last],
                            [everyone], q_parts[family][first:last], trans, slots))
    stats = jnp.concatenate(results, axis=0)[:, :4, :]
    blocks = [stats[:, :, place * rows:(place + 1) * rows] for place in range(share)]
    spread = jnp.stack(blocks, axis=0)
    me = pose % share
    own = []
    for member in range(share):
        block = lax.dynamic_index_in_dim(spread, me ^ member, 0, keepdims=False)
        block = swap(block, "pose", member) if member else block
        own += [(member, spot, block[spot]) for spot in range(families * local)]

    cand = candidates.T
    owner = cand // local
    beyond = (owner ^ pose) // share
    within = (owner ^ pose) % share
    position = beyond * local + cand % local
    picked = jnp.zeros((picks, 4, rows), jnp.float32)
    for member, spot, block in own:
        hit = (within == member) & (position == spot)
        picked = jnp.where(hit[:, None, :], block[None], picked)
    log_weight = picked[:, 0] + jnp.log(picked[:, 1])
    raw_weight = jnp.exp(log_weight - jnp.max(log_weight, axis=0, keepdims=True))
    class_prob = raw_weight / jnp.sum(raw_weight, axis=0, keepdims=True)
    mean_x = jnp.sum(class_prob * picked[:, 2] / picked[:, 1], axis=0)
    mean_y = jnp.sum(class_prob * picked[:, 3] / picked[:, 1], axis=0)
    return (class_prob.T, jnp.stack([mean_x, mean_y], axis=1))


def solution(mesh):
    in_specs = (
        P(("pose", "dom"), None),
        P(("pose", "dom"), None),
        P(("pose", "dom")),
        P(("pose", "dom"), None, None),
        P(),
        P(),
        P("pose", "dom", None),
    )
    out_specs = (P(("pose", "dom"), None), P(("pose", "dom"), None))
    return jax.shard_map(
        on_device, mesh=mesh, in_specs=in_specs, out_specs=out_specs, check_vma=False
    )
```

```python
import functools

import jax
import jax.numpy as jnp
import ml_dtypes
import numpy as np
from jax import lax
from jax.experimental import pallas as pl
from jax.experimental.pallas import tpu as pltpu
from jax.sharding import PartitionSpec as P

BOX = 128
GRID_X = 64
REACH = 3
SHARE = 4
TILE = 32
CHUNK = 512
LANES = 128
STRIDE = 4
HALF = 16
HIGHEST = lax.Precision.HIGHEST


def split_three(values):
    parts = []
    for _ in range(3):
        part = lax.reduce_precision(values, 8, 7)
        parts.append(part.astype(jnp.bfloat16))
        values = values - part
    return parts


def phase_table(pixel_count):
    levels = np.arange(-REACH, REACH + 1)
    starts = np.arange(0, pixel_count, STRIDE * LANES)
    pixel = starts[:, None] + np.arange(LANES)[None, :]
    shift_x = np.repeat(levels, levels.size)[:, None, None]
    shift_y = np.tile(levels, levels.size)[:, None, None]
    angle = shift_x * (pixel % GRID_X - GRID_X // 2) + shift_y * (pixel // GRID_X)
    onward = np.broadcast_to(shift_y * (LANES // GRID_X), (levels.size**2, 1, LANES))
    angle = 2.0 * np.pi / BOX * np.concatenate([angle, onward], axis=1)
    rest = np.stack([np.cos(angle), np.sin(angle)], axis=2).reshape(levels.size**2, -1).astype(np.float32)
    parts = []
    for _ in range(3):
        part = rest.astype(ml_dtypes.bfloat16)
        parts.append(part)
        rest = rest - part.astype(np.float32)
    rows = np.concatenate(parts, axis=0)
    count = levels.size**2
    padded = np.zeros((256, rows.shape[1]), ml_dtypes.bfloat16)
    padded[: rows.shape[0]] = rows
    label = np.full((1, 256), -1.0, np.float32)
    label[0, : rows.shape[0]] = np.arange(rows.shape[0]) % count
    return (padded, label)


def swap(values, axis, bit):
    count = lax.axis_size(axis)
    return lax.ppermute(values, axis, [(index, index ^ bit) for index in range(count)])


def stats_kernel(trans, spots, share, tiles_ref, rank_ref, meta_ref, label_ref, table_ref, wtab_ref,
                 dtab_ref, *refs):
    classes, pieces = len(spots), len(spots[0])
    x_refs = refs[:share]
    q_refs = refs[share:share + classes * pieces]
    (out_ref, parts, proj, uv, pens, info, stats, phase, shifted, x_sem,
     q_sem) = refs[share + classes * pieces:]
    rows_x = x_refs[0].shape[0]
    rows_q = q_refs[0].shape[1]
    rows_all = parts.shape[0]
    slots = uv.shape[0] // classes
    pixels = uv.shape[1] // 2
    ori = proj.shape[1]
    groups = dtab_ref.shape[0] // 3
    contract = (((1,), (1,)), ((), ()))

    x_copies = [
        pltpu.make_async_copy(x_refs[index], parts.at[pl.ds(index * rows_x, rows_x)], x_sem.at[index])
        for index in range(share)
    ]
    q_copies = [
        pltpu.make_async_copy(q_refs[place * pieces + index].at[spots[place][index]],
                              proj.at[place, pl.ds(index * rows_q, rows_q)], q_sem.at[place, index])
        for place in range(classes)
        for index in range(pieces)
    ]
    for copy in x_copies + q_copies:
        copy.start()

    row = lax.broadcasted_iota(jnp.int32, (slots, rows_all), 0)
    pick = jnp.concatenate(
        [jnp.where(rank_ref[place:place + 1, :] == row, 1.0, 0.0) for place in range(classes)], axis=0
    ).astype(jnp.bfloat16)
    info[...] = jnp.dot(pick, meta_ref[...], preferred_element_type=jnp.float32)
    lane = lax.broadcasted_iota(jnp.int32, (classes * slots, 128), 1)
    group_hot = jnp.where(info[:, trans:trans + 1] == (lane % groups).astype(jnp.float32), 1.0, 0.0)
    group_bf = jnp.where(lane < 3 * groups, group_hot, 0.0).astype(jnp.bfloat16)
    stats[...] = jnp.zeros_like(stats)
    for copy in x_copies:
        copy.wait()
    for first in range(0, pixels, CHUNK):
        weight = jnp.dot(group_bf, wtab_ref[:, first:first + CHUNK], preferred_element_type=jnp.float32)
        for start in (first, pixels + first):
            rows = jnp.dot(pick, parts[:, start:start + CHUNK], preferred_element_type=jnp.float32)
            uv[:, start:start + CHUNK] = weight * rows
    for copy in q_copies:
        copy.wait()

    label = label_ref[...]
    lanes = lax.broadcasted_iota(jnp.int32, (TILE, 128), 1)
    steps = pixels // LANES

    @pl.loop(0, classes)
    def _(place):
        parted = jnp.zeros((3 * groups, ori), jnp.float32)
        for first in range(0, pixels, CHUNK):
            real = proj[place, :, first:first + CHUNK].astype(jnp.float32)
            imag = proj[place, :, pixels + first:pixels + first + CHUNK].astype(jnp.float32)
            power = real * real + imag * imag
            high = power.astype(jnp.bfloat16)
            low = (power - high.astype(jnp.float32)).astype(jnp.bfloat16)
            for part in (high, low):
                parted += lax.dot_general(dtab_ref[:, first:first + CHUNK], part, contract,
                                          preferred_element_type=jnp.float32)
        penalty = -0.5 * (parted[:groups] + parted[groups:2 * groups] + parted[2 * groups:])
        base = pl.multiple_of(place * slots, TILE)
        mine = pl.ds(base, slots)
        mine_lane = lax.broadcasted_iota(jnp.int32, (slots, groups), 1).astype(jnp.float32)
        mine_hot = jnp.where(info[mine, trans:trans + 1] == mine_lane, 1.0, 0.0)
        pens[...] = jnp.dot(mine_hot, penalty, precision=HIGHEST, preferred_element_type=jnp.float32)

        @pl.loop(0, tiles_ref[place])
        def _(tile):
            start = pl.multiple_of(base + tile * TILE, TILE)
            here = info[pl.ds(start, TILE), :]
            hot = jnp.concatenate(
                [jnp.where(here[:, t:t + 1] == label, 1.0, 0.0) for t in range(trans)], axis=0
            ).astype(jnp.bfloat16)
            phase[...] = jnp.dot(hot, table_ref[...], preferred_element_type=jnp.float32)
            scores = jnp.zeros((trans * TILE, ori), jnp.float32)
            onward = 2 * LANES * (steps // STRIDE)
            for group in range(steps // STRIDE):
                for first in range(0, trans * TILE, HALF):
                    rows = slice(first, first + HALF)
                    source = pl.ds(pl.multiple_of(start + first % TILE, HALF), HALF)
                    cosine = phase[rows, 2 * LANES * group:2 * LANES * group + LANES]
                    sine = phase[rows, 2 * LANES * group + LANES:2 * LANES * (group + 1)]
                    turn_c = phase[rows, onward:onward + LANES]
                    turn_s = phase[rows, onward + LANES:onward + 2 * LANES]
                    for step in range(STRIDE):
                        at = (group * STRIDE + step) * LANES
                        real = uv[source, at:at + LANES]
                        imag = uv[source, pixels + at:pixels + at + LANES]
                        shifted[rows, at:at + LANES] = (real * cosine + imag * sine).astype(jnp.bfloat16)
                        shifted[rows, pixels + at:pixels + at + LANES] = (
                            imag * cosine - real * sine).astype(jnp.bfloat16)
                        if step < STRIDE - 1:
                            cosine, sine = (cosine * turn_c - sine * turn_s,
                                            sine * turn_c + cosine * turn_s)
                width = STRIDE * LANES
                for at in (group * width, pixels + group * width):
                    scores += lax.dot_general(shifted[:, at:at + width], proj[place, :, at:at + width],
                                              contract, preferred_element_type=jnp.float32)
            local = pl.multiple_of(tile * TILE, TILE)
            full = scores.reshape(trans, TILE, ori) + pens[pl.ds(local, TILE), :][None]
            highest = jnp.max(jnp.max(full, axis=0), axis=1, keepdims=True)
            total = jnp.zeros((TILE, ori), jnp.float32)
            moment_x = jnp.zeros((TILE, ori), jnp.float32)
            moment_y = jnp.zeros((TILE, ori), jnp.float32)
            for t in range(trans):
                term = jnp.exp(full[t] - highest)
                total += term
                moment_x += term * here[:, trans + 1 + t:trans + 2 + t]
                moment_y += term * here[:, 2 * trans + 1 + t:2 * trans + 2 + t]
            total = jnp.sum(total, axis=1, keepdims=True)
            moment_x = jnp.sum(moment_x, axis=1, keepdims=True)
            moment_y = jnp.sum(moment_y, axis=1, keepdims=True)
            stats[pl.ds(start, TILE), :] = jnp.where(
                lanes == 0, highest,
                jnp.where(lanes == 1, total, jnp.where(lanes == 2, moment_x,
                                                       jnp.where(lanes == 3, moment_y, 0.0))))

    for place in range(classes):
        mine = slice(place * slots, (place + 1) * slots)
        back = lax.dot_general(stats[mine, :], pick[mine, :].astype(jnp.float32), (((0,), (0,)), ((), ())),
                               precision=HIGHEST, preferred_element_type=jnp.float32)
        out_ref[place] = back[:8, :]


def class_stats(tiles, rank, meta, label, table, wtab, dtab, x_parts, q_parts, trans, slots):
    classes, rows_all = rank.shape
    share, pieces = len(x_parts), len(q_parts[0])
    rows_q, width = q_parts[0][0][0].shape[1:]
    ori = rows_q * pieces
    flat = [array for members in q_parts for array, _ in members]
    spots = [[spot for _, spot in members] for members in q_parts]
    vmem = pl.BlockSpec(memory_space=pltpu.VMEM)
    anywhere = pl.BlockSpec(memory_space=pl.ANY)
    return pl.pallas_call(
        functools.partial(stats_kernel, trans, spots, share),
        out_shape=jax.ShapeDtypeStruct((classes, 8, rows_all), jnp.float32),
        in_specs=[pl.BlockSpec(memory_space=pltpu.SMEM)] + [vmem] * 6 + [anywhere] * (share + len(flat)),
        out_specs=vmem,
        scratch_shapes=[
            pltpu.VMEM((rows_all, width), jnp.bfloat16),
            pltpu.VMEM((classes, ori, width), jnp.bfloat16),
            pltpu.VMEM((classes * slots, width), jnp.float32),
            pltpu.VMEM((slots, ori), jnp.float32),
            pltpu.VMEM((classes * slots, 128), jnp.float32),
            pltpu.VMEM((classes * slots, 128), jnp.float32),
            pltpu.VMEM((trans * TILE, table.shape[1]), jnp.float32),
            pltpu.VMEM((trans * TILE, width), jnp.bfloat16),
            pltpu.SemaphoreType.DMA((share,)),
            pltpu.SemaphoreType.DMA((classes, pieces)),
        ],
        compiler_params=pltpu.CompilerParams(vmem_limit_bytes=40 * 1024 * 1024),
        cost_estimate=pl.CostEstimate(
            flops=20 * classes * slots * trans * width * (ori + 256),
            bytes_accessed=(rows_all + classes * ori) * width * 2,
            transcendentals=0,
        ),
    )(tiles, rank, meta, label, table, wtab, dtab, *x_parts, *flat)


def on_device(particles, candidates, ctf_ids, offsets, ctf_table, sigma_sq, projections):
    pose_count = lax.axis_size("pose")
    dom_count = lax.axis_size("dom")
    pose = lax.axis_index("pose")
    local = projections.shape[0]
    class_total = local * pose_count
    rows, picks = candidates.shape
    trans = offsets.shape[2]
    pixels = sigma_sq.shape[0]
    capacity = 3 * rows * picks // class_total
    share = min(SHARE, pose_count)
    share_bits = [1 << b for b in range(share.bit_length() - 1)]
    families = pose_count // share
    slots = -(-min(share * capacity, share * rows) // TILE) * TILE

    x_parts, order = [particles], [0]
    for bit in share_bits[::-1]:
        x_parts = x_parts + [swap(member, "pose", bit) for member in x_parts]
        order = order + [member ^ bit for member in order]

    dom_bits = [1 << b for b in range(dom_count.bit_length() - 1)][::-1]

    def over_dom(array):
        members = [array]
        for bit in dom_bits:
            members = members + [swap(member, "dom", bit) for member in members]
        return members

    q_parts = []
    own_pieces = over_dom(projections)
    q_parts.append([[(piece, spot) for piece in own_pieces] for spot in range(local)])
    for family in range(1, families):
        members = []
        for spot in range(local):
            piece = swap(projections[spot:spot + 1], "pose", family * share)
            members.append([(member, 0) for member in over_dom(piece)])
        q_parts.append(members)

    offsets, candidates_late, _ = lax.optimization_barrier((offsets, candidates, x_parts[1]))
    offset_f = offsets.astype(jnp.float32)
    combo = (offset_f[:, 0] + REACH) * (2 * REACH + 1) + (offset_f[:, 1] + REACH)
    meta = jnp.concatenate(
        [combo, ctf_ids[:, None].astype(jnp.float32), offset_f[:, 0], offset_f[:, 1],
         candidates_late.astype(jnp.float32)], axis=1)
    meta = jnp.pad(meta, ((0, 0), (0, 128 - meta.shape[1]))).astype(jnp.bfloat16)
    metas = [swap(meta, "pose", member) if member else meta for member in order]
    meta_all = jnp.concatenate(metas, axis=0)

    weight = ctf_table / sigma_sq[None, :]
    wtab = jnp.concatenate(split_three(weight), axis=0)
    wtab = jnp.pad(wtab, ((0, 128 - wtab.shape[0]), (0, 0)))
    dtab = jnp.concatenate(split_three(weight * ctf_table), axis=0)

    named = meta_all[:, 3 * trans + 1:3 * trans + 1 + picks].astype(jnp.int32)
    owner = pose ^ (jnp.arange(families, dtype=jnp.int32) * share)
    class_ids = (owner[:, None] * local + jnp.arange(local, dtype=jnp.int32)[None, :]).reshape(-1)
    names = jnp.any(named.T[None, :, :] == class_ids[:, None, None], axis=1).astype(jnp.int32)
    ahead = jnp.cumsum(names, axis=1)
    rank = jnp.where(names > 0, ahead - 1, -1)
    tiles = (ahead[:, -1] + (TILE - 1)) // TILE

    table, label = phase_table(pixels)
    table, label = jnp.asarray(table), jnp.asarray(label)
    results = []
    for family in range(families):
        spans = [(0, local)] if family == 0 else [(spot, spot + 1) for spot in range(local)]
        for first, last in spans:
            span = slice(family * local + first, family * local + last)
            if results:
                tiles, results[-1] = lax.optimization_barrier((tiles, results[-1]))
            results.append(
                class_stats(tiles[span], rank[span], meta_all, label, table, wtab, dtab,
                            x_parts, q_parts[family][first:last], trans, slots))
    stats = jnp.concatenate(results, axis=0)[:, :4, :]
    own = []
    for place, member in enumerate(order):
        block = stats[:, :, place * rows:(place + 1) * rows]
        block = swap(block, "pose", member) if member else block
        own += [(member, spot, block[spot]) for spot in range(families * local)]

    cand = candidates.T
    owner = cand // local
    beyond = (owner ^ pose) // share
    within = (owner ^ pose) % share
    position = beyond * local + cand % local
    picked = jnp.zeros((picks, 4, rows), jnp.float32)
    for member, spot, block in own:
        hit = (within == member) & (position == spot)
        picked = jnp.where(hit[:, None, :], block[None], picked)
    log_weight = picked[:, 0] + jnp.log(picked[:, 1])
    raw_weight = jnp.exp(log_weight - jnp.max(log_weight, axis=0, keepdims=True))
    class_prob = raw_weight / jnp.sum(raw_weight, axis=0, keepdims=True)
    mean_x = jnp.sum(class_prob * picked[:, 2] / picked[:, 1], axis=0)
    mean_y = jnp.sum(class_prob * picked[:, 3] / picked[:, 1], axis=0)
    return (class_prob.T, jnp.stack([mean_x, mean_y], axis=1))


def solution(mesh):
    in_specs = (
        P(("pose", "dom"), None),
        P(("pose", "dom"), None),
        P(("pose", "dom")),
        P(("pose", "dom"), None, None),
        P(),
        P(),
        P("pose", "dom", None),
    )
    out_specs = (P(("pose", "dom"), None), P(("pose", "dom"), None))
    return jax.shard_map(
        on_device, mesh=mesh, in_specs=in_specs, out_specs=out_specs, check_vma=False
    )
```

```python
import functools

import jax
import jax.numpy as jnp
import ml_dtypes
import numpy as np
from jax import lax
from jax.experimental import pallas as pl
from jax.experimental.pallas import tpu as pltpu
from jax.sharding import PartitionSpec as P

BOX = 128
GRID_X = 64
REACH = 3
SHARE = 4
TILE = 32
CHUNK = 512
LANES = 128
STRIDE = 4
HIGHEST = lax.Precision.HIGHEST


def split_three(values):
    parts = []
    for _ in range(3):
        part = lax.reduce_precision(values, 8, 7)
        parts.append(part.astype(jnp.bfloat16))
        values = values - part
    return parts


def phase_table(pixel_count):
    levels = np.arange(-REACH, REACH + 1)
    starts = np.arange(0, pixel_count, STRIDE * LANES)
    pixel = starts[:, None] + np.arange(LANES)[None, :]
    shift_x = np.repeat(levels, levels.size)[:, None, None]
    shift_y = np.tile(levels, levels.size)[:, None, None]
    angle = shift_x * (pixel % GRID_X - GRID_X // 2) + shift_y * (pixel // GRID_X)
    onward = np.broadcast_to(shift_y * (LANES // GRID_X), (levels.size**2, 1, LANES))
    angle = 2.0 * np.pi / BOX * np.concatenate([angle, onward], axis=1)
    rest = np.stack([np.cos(angle), np.sin(angle)], axis=2).reshape(levels.size**2, -1).astype(np.float32)
    parts = []
    for _ in range(3):
        part = rest.astype(ml_dtypes.bfloat16)
        parts.append(part)
        rest = rest - part.astype(np.float32)
    rows = np.concatenate(parts, axis=0)
    count = levels.size**2
    padded = np.zeros((256, rows.shape[1]), ml_dtypes.bfloat16)
    padded[: rows.shape[0]] = rows
    label = np.full((1, 256), -1.0, np.float32)
    label[0, : rows.shape[0]] = np.arange(rows.shape[0]) % count
    return (padded, label)


def swap(values, axis, bit):
    count = lax.axis_size(axis)
    return lax.ppermute(values, axis, [(index, index ^ bit) for index in range(count)])


def stats_kernel(trans, spots, share, tiles_ref, rank_ref, meta_ref, label_ref, table_ref, wtab_ref,
                 dtab_ref, *refs):
    x_refs = refs[:share]
    q_refs = refs[share:share + len(spots)]
    out_ref, uv, pens, info, stats, phase, shifted, moved = refs[share + len(spots):]
    rows_all = rank_ref.shape[1]
    slots = uv.shape[0]
    pixels = uv.shape[1] // 2
    ori = pens.shape[1]
    groups = dtab_ref.shape[0] // 3
    contract = (((1,), (1,)), ((), ()))

    def particles(cols):
        return jnp.concatenate([member[:, cols] for member in x_refs], axis=0)

    def views(cols):
        return jnp.concatenate([member[spot, :, cols] for member, spot in zip(q_refs, spots)], axis=0)

    def three(values):
        high = values.astype(jnp.bfloat16)
        rest = values - high.astype(jnp.float32)
        middle = rest.astype(jnp.bfloat16)
        return [high, middle, (rest - middle.astype(jnp.float32)).astype(jnp.bfloat16)]

    row = lax.broadcasted_iota(jnp.int32, (slots, rows_all), 0)
    pick = jnp.where(rank_ref[...] == row, 1.0, 0.0).astype(jnp.bfloat16)
    info[...] = jnp.dot(pick, meta_ref[...], preferred_element_type=jnp.float32)
    lane = lax.broadcasted_iota(jnp.int32, (slots, 3 * groups), 1)
    group_hot = jnp.where(info[:, trans:trans + 1] == (lane % groups).astype(jnp.float32), 1.0, 0.0)
    group_hot = group_hot.astype(jnp.bfloat16)
    stats[...] = jnp.zeros_like(stats)
    parted = jnp.zeros((3 * groups, ori), jnp.float32)
    for first in range(0, pixels, CHUNK):
        cols, icols = slice(first, first + CHUNK), slice(pixels + first, pixels + first + CHUNK)
        weight = jnp.dot(group_hot, wtab_ref[:, cols], preferred_element_type=jnp.float32)
        for span in (cols, icols):
            uv[:, span] = weight * jnp.dot(pick, particles(span), preferred_element_type=jnp.float32)
        real = views(cols).astype(jnp.float32)
        imag = views(icols).astype(jnp.float32)
        power = real * real + imag * imag
        for part in three(power)[:2]:
            parted += lax.dot_general(dtab_ref[:, cols], part, contract, preferred_element_type=jnp.float32)
    penalty = -0.5 * (parted[:groups] + parted[groups:2 * groups] + parted[2 * groups:])
    pens[...] = jnp.dot(group_hot, jnp.concatenate(three(penalty), axis=0),
                        preferred_element_type=jnp.float32)

    label = label_ref[...]
    lanes = lax.broadcasted_iota(jnp.int32, (TILE, 128), 1)
    steps = pixels // LANES

    @pl.loop(0, tiles_ref[0])
    def _(tile):
        mine = pl.ds(pl.multiple_of(tile * TILE, TILE), TILE)
        here = info[mine, :]
        moved[...] = uv[mine, :]
        penalties = pens[mine, :]
        hot = jnp.concatenate(
            [jnp.where(here[:, t:t + 1] == label, 1.0, 0.0) for t in range(trans)], axis=0
        ).astype(jnp.bfloat16)
        phase[...] = jnp.dot(hot, table_ref[...], preferred_element_type=jnp.float32)
        scores = jnp.zeros((trans * TILE, ori), jnp.float32)
        onward = 2 * LANES * (steps // STRIDE)
        for group in range(steps // STRIDE):
            for t in range(trans):
                rows = slice(t * TILE, (t + 1) * TILE)
                cosine = phase[rows, 2 * LANES * group:2 * LANES * group + LANES]
                sine = phase[rows, 2 * LANES * group + LANES:2 * LANES * (group + 1)]
                turn_c = phase[rows, onward:onward + LANES]
                turn_s = phase[rows, onward + LANES:onward + 2 * LANES]
                for step in range(STRIDE):
                    at = (group * STRIDE + step) * LANES
                    real = moved[:, at:at + LANES]
                    imag = moved[:, pixels + at:pixels + at + LANES]
                    shifted[rows, at:at + LANES] = (real * cosine + imag * sine).astype(jnp.bfloat16)
                    shifted[rows, pixels + at:pixels + at + LANES] = (
                        imag * cosine - real * sine).astype(jnp.bfloat16)
                    if step < STRIDE - 1:
                        cosine, sine = (cosine * turn_c - sine * turn_s,
                                        sine * turn_c + cosine * turn_s)
            width = STRIDE * LANES
            for at in (group * width, pixels + group * width):
                span = slice(at, at + width)
                scores += lax.dot_general(shifted[:, span], views(span), contract,
                                          preferred_element_type=jnp.float32)
        full = scores.reshape(trans, TILE, ori) + penalties[None]
        highest = jnp.max(jnp.max(full, axis=0), axis=1, keepdims=True)
        total = jnp.zeros((TILE, ori), jnp.float32)
        moment_x = jnp.zeros((TILE, ori), jnp.float32)
        moment_y = jnp.zeros((TILE, ori), jnp.float32)
        for t in range(trans):
            term = jnp.exp(full[t] - highest)
            total += term
            moment_x += term * here[:, trans + 1 + t:trans + 2 + t]
            moment_y += term * here[:, 2 * trans + 1 + t:2 * trans + 2 + t]
        total = jnp.sum(total, axis=1, keepdims=True)
        moment_x = jnp.sum(moment_x, axis=1, keepdims=True)
        moment_y = jnp.sum(moment_y, axis=1, keepdims=True)
        stats[mine, :] = jnp.where(
            lanes == 0, highest,
            jnp.where(lanes == 1, total, jnp.where(lanes == 2, moment_x,
                                                   jnp.where(lanes == 3, moment_y, 0.0))))

    back = sum(
        lax.dot_general(part, pick, (((0,), (0,)), ((), ())), preferred_element_type=jnp.float32)
        for part in three(stats[...])
    )
    out_ref[0] = back[:8, :]


def class_stats(tiles, rank, meta, label, table, wtab, dtab, x_parts, q_parts, trans, slots):
    rows_all = rank.shape[1]
    rows_q, width = q_parts[0][0].shape[1:]
    ori = rows_q * len(q_parts)
    arrays = [array for array, _ in q_parts]
    spots = [spot for _, spot in q_parts]
    vmem = pl.BlockSpec(memory_space=pltpu.VMEM)
    return pl.pallas_call(
        functools.partial(stats_kernel, trans, spots, len(x_parts)),
        out_shape=jax.ShapeDtypeStruct((1, 8, rows_all), jnp.float32),
        in_specs=[pl.BlockSpec(memory_space=pltpu.SMEM)] + [vmem] * (6 + len(x_parts) + len(arrays)),
        out_specs=vmem,
        scratch_shapes=[
            pltpu.VMEM((slots, width), jnp.float32),
            pltpu.VMEM((slots, ori), jnp.float32),
            pltpu.VMEM((slots, 128), jnp.float32),
            pltpu.VMEM((slots, 128), jnp.float32),
            pltpu.VMEM((trans * TILE, table.shape[1]), jnp.float32),
            pltpu.VMEM((trans * TILE, width), jnp.bfloat16),
            pltpu.VMEM((TILE, width), jnp.float32),
        ],
        compiler_params=pltpu.CompilerParams(vmem_limit_bytes=36 * 1024 * 1024),
        cost_estimate=pl.CostEstimate(
            flops=20 * slots * trans * width * (ori + 256),
            bytes_accessed=(rows_all + ori) * width * 2,
            transcendentals=0,
        ),
    )(tiles, rank, meta, label, table, wtab, dtab, *x_parts, *arrays)


def on_device(particles, candidates, ctf_ids, offsets, ctf_table, sigma_sq, projections):
    pose_count = lax.axis_size("pose")
    dom_count = lax.axis_size("dom")
    pose = lax.axis_index("pose")
    local = projections.shape[0]
    class_total = local * pose_count
    rows, picks = candidates.shape
    trans = offsets.shape[2]
    pixels = sigma_sq.shape[0]
    capacity = 3 * rows * picks // class_total
    share = min(SHARE, pose_count)
    share_bits = [1 << b for b in range(share.bit_length() - 1)]
    families = pose_count // share
    slots = -(-min(share * capacity, share * rows) // TILE) * TILE

    dom_bits = [1 << b for b in range(dom_count.bit_length() - 1)][::-1]

    offset_f = offsets.astype(jnp.float32)
    combo = (offset_f[:, 0] + REACH) * (2 * REACH + 1) + (offset_f[:, 1] + REACH)
    meta = jnp.concatenate(
        [combo, ctf_ids[:, None].astype(jnp.float32), offset_f[:, 0], offset_f[:, 1],
         candidates.astype(jnp.float32)], axis=1)
    meta = jnp.pad(meta, ((0, 0), (0, 128 - meta.shape[1]))).astype(jnp.bfloat16)

    order = [0]
    for bit in share_bits[::-1]:
        order = order + [member ^ bit for member in order]
    single = {bit: swap(particles, "pose", bit) for bit in share_bits[::-1]}
    own_pieces = [projections] + [swap(projections, "dom", bit) for bit in dom_bits[:1]]
    metas = [swap(meta, "pose", member) if member else meta for member in order]
    chunks = [projections[spot:spot + 1] for spot in range(local)]
    meta_all = jnp.concatenate(metas, axis=0)

    named = meta_all[:, 3 * trans + 1:3 * trans + 1 + picks].astype(jnp.int32)
    owner = pose ^ (jnp.arange(families, dtype=jnp.int32) * share)
    class_ids = (owner[:, None] * local + jnp.arange(local, dtype=jnp.int32)[None, :]).reshape(-1)
    names = jnp.any(named.T[None, :, :] == class_ids[:, None, None], axis=1).astype(jnp.int32)
    ahead = jnp.cumsum(names, axis=1)
    rank = jnp.where(names > 0, ahead - 1, -1)
    tiles = (ahead[:, -1] + (TILE - 1)) // TILE

    single, own_pieces, chunks, rank, tiles = lax.optimization_barrier(
        (single, own_pieces, chunks, rank, tiles))

    x_parts = []
    for member in order:
        bits = [bit for bit in share_bits if member & bit]
        part = single[bits[-1]] if bits else particles
        for bit in bits[:-1]:
            part = swap(part, "pose", bit)
        x_parts.append(part)

    def over_dom(members, bits):
        for bit in bits:
            members = members + [swap(member, "dom", bit) for member in members]
        return members

    far = [[swap(chunks[spot], "pose", family * share) for spot in range(local)]
           for family in range(1, families)]
    own_pieces = over_dom(own_pieces, dom_bits[1:])
    weight = ctf_table / sigma_sq[None, :]
    wtab = jnp.concatenate(split_three(weight), axis=0)
    dtab = jnp.concatenate(split_three(weight * ctf_table), axis=0)

    table, label = phase_table(pixels)
    table, label = jnp.asarray(table), jnp.asarray(label)
    results = []

    def one_class(index, members):
        turn = tiles[index:index + 1]
        if results:
            turn, results[-1] = lax.optimization_barrier((turn, results[-1]))
        results.append(class_stats(turn, rank[index:index + 1], meta_all, label, table, wtab, dtab,
                                   x_parts, members, trans, slots))

    for spot in range(local):
        one_class(spot, [(piece, spot) for piece in own_pieces])
    for family in range(1, families):
        for spot in range(local):
            pieces = [far[family - 1][spot]]
            for hop, bit in enumerate(dom_bits):
                if spot:
                    tie = -1 if hop else spot
                    pieces[hop:], results[tie] = lax.optimization_barrier((pieces[hop:], results[tie]))
                pieces = pieces + [swap(member, "dom", bit) for member in pieces]
            one_class(family * local + spot, [(member, 0) for member in pieces])
    stats = jnp.concatenate(results, axis=0)[:, :4, :]
    own = []
    for place, member in enumerate(order):
        block = stats[:, :, place * rows:(place + 1) * rows]
        block = swap(block, "pose", member) if member else block
        own += [(member, spot, block[spot]) for spot in range(families * local)]

    cand = candidates.T
    owner = cand // local
    beyond = (owner ^ pose) // share
    within = (owner ^ pose) % share
    position = beyond * local + cand % local
    picked = jnp.zeros((picks, 4, rows), jnp.float32)
    for member, spot, block in own:
        hit = (within == member) & (position == spot)
        picked = jnp.where(hit[:, None, :], block[None], picked)
    log_weight = picked[:, 0] + jnp.log(picked[:, 1])
    raw_weight = jnp.exp(log_weight - jnp.max(log_weight, axis=0, keepdims=True))
    class_prob = raw_weight / jnp.sum(raw_weight, axis=0, keepdims=True)
    mean_x = jnp.sum(class_prob * picked[:, 2] / picked[:, 1], axis=0)
    mean_y = jnp.sum(class_prob * picked[:, 3] / picked[:, 1], axis=0)
    return (class_prob.T, jnp.stack([mean_x, mean_y], axis=1))


def solution(mesh):
    in_specs = (
        P(("pose", "dom"), None),
        P(("pose", "dom"), None),
        P(("pose", "dom")),
        P(("pose", "dom"), None, None),
        P(),
        P(),
        P("pose", "dom", None),
    )
    out_specs = (P(("pose", "dom"), None), P(("pose", "dom"), None))
    return jax.shard_map(
        on_device, mesh=mesh, in_specs=in_specs, out_specs=out_specs, check_vma=False
    )
```

```python
import functools

import jax
import jax.numpy as jnp
import ml_dtypes
import numpy as np
from jax import lax
from jax.experimental import pallas as pl
from jax.experimental.pallas import tpu as pltpu
from jax.sharding import PartitionSpec as P

BOX = 128
GRID_X = 64
REACH = 3
SHARE = 4
TILE = 32
HALF = 16
CHUNK = 512
PIECE = 256
HIGHEST = lax.Precision.HIGHEST


def split_three(values):
    parts = []
    for _ in range(3):
        part = lax.reduce_precision(values, 8, 7)
        parts.append(part.astype(jnp.bfloat16))
        values = values - part
    return parts


def phase_table(pixel_count):
    levels = np.arange(-REACH, REACH + 1)
    pixel = np.arange(pixel_count).reshape(-1, PIECE)
    shift_x = np.repeat(levels, levels.size)[:, None, None]
    shift_y = np.tile(levels, levels.size)[:, None, None]
    angle = 2.0 * np.pi / BOX * (
        shift_x * (pixel % GRID_X - GRID_X // 2) + shift_y * (pixel // GRID_X))
    rest = np.stack([np.cos(angle), np.sin(angle)], axis=2).reshape(levels.size**2, -1).astype(np.float32)
    parts = []
    for _ in range(3):
        part = rest.astype(ml_dtypes.bfloat16)
        parts.append(part)
        rest = rest - part.astype(np.float32)
    rows = np.concatenate(parts, axis=0)
    count = levels.size**2
    padded = np.zeros((256, rows.shape[1]), ml_dtypes.bfloat16)
    padded[: rows.shape[0]] = rows
    label = np.full((1, 256), -1.0, np.float32)
    label[0, : rows.shape[0]] = np.arange(rows.shape[0]) % count
    return (padded, label)


def swap(values, axis, bit):
    count = lax.axis_size(axis)
    return lax.ppermute(values, axis, [(index, index ^ bit) for index in range(count)])


def three(values):
    high = values.astype(jnp.bfloat16)
    rest = values - high.astype(jnp.float32)
    middle = rest.astype(jnp.bfloat16)
    return [high, middle, (rest - middle.astype(jnp.float32)).astype(jnp.bfloat16)]


contract_last = (((1,), (1,)), ((), ()))


def penalties_of(views, dtab_ref, ori, pixels):
    groups = dtab_ref.shape[0] // 3
    parted = jnp.zeros((3 * groups, ori), jnp.float32)
    for first in range(0, pixels, CHUNK):
        real = views(slice(first, first + CHUNK)).astype(jnp.float32)
        imag = views(slice(pixels + first, pixels + first + CHUNK)).astype(jnp.float32)
        for part in three(real * real + imag * imag)[:2]:
            parted += lax.dot_general(dtab_ref[:, first:first + CHUNK], part, contract_last,
                                      preferred_element_type=jnp.float32)
    return -0.5 * (parted[:groups] + parted[groups:2 * groups] + parted[2 * groups:])


def views_of(q_refs, spots):
    def views(cols):
        return jnp.concatenate([member[spot, :, cols] for member, spot in zip(q_refs, spots)], axis=0)
    return views


def penalty_kernel(pieces, dtab_ref, *refs):
    out_ref = refs[pieces]
    for place in range(out_ref.shape[0]):
        views = views_of(refs[:pieces], [place] * pieces)
        out_ref[place] = penalties_of(views, dtab_ref, out_ref.shape[2], dtab_ref.shape[1])


def own_penalties(dtab, pieces):
    classes, rows_q, width = pieces[0].shape
    ori = rows_q * len(pieces)
    vmem = pl.BlockSpec(memory_space=pltpu.VMEM)
    return pl.pallas_call(
        functools.partial(penalty_kernel, len(pieces)),
        out_shape=jax.ShapeDtypeStruct((classes, dtab.shape[0] // 3, ori), jnp.float32),
        in_specs=[vmem] * (1 + len(pieces)),
        out_specs=vmem,
        compiler_params=pltpu.CompilerParams(vmem_limit_bytes=24 * 1024 * 1024),
    )(dtab, *pieces)


def stats_kernel(trans, spots, share, have_penalty, tiles_ref, rank_ref, meta_ref, label_ref, table_ref,
                 wtab_ref, dtab_ref, *refs):
    if have_penalty:
        penalty_ref, refs = refs[0], refs[1:]
    x_refs = refs[:share]
    q_refs = refs[share:share + len(spots)]
    out_ref, uv, pens, info, stats, shifted = refs[share + len(spots):]
    rows_all = rank_ref.shape[1]
    slots = uv.shape[0]
    pixels = uv.shape[1] // 2
    ori = pens.shape[1]
    groups = dtab_ref.shape[0] // 3
    views = views_of(q_refs, spots)

    def particles(cols):
        return jnp.concatenate([member[:, cols] for member in x_refs], axis=0)

    row = lax.broadcasted_iota(jnp.int32, (slots, rows_all), 0)
    pick = jnp.where(rank_ref[...] == row, 1.0, 0.0).astype(jnp.bfloat16)
    info[...] = jnp.dot(pick, meta_ref[...], preferred_element_type=jnp.float32)
    lane = lax.broadcasted_iota(jnp.int32, (slots, 3 * groups), 1)
    group_hot = jnp.where(info[:, trans:trans + 1] == (lane % groups).astype(jnp.float32), 1.0, 0.0)
    group_hot = group_hot.astype(jnp.bfloat16)
    stats[...] = jnp.zeros_like(stats)
    for first in range(0, pixels, CHUNK):
        weight = jnp.dot(group_hot, wtab_ref[:, first:first + CHUNK], preferred_element_type=jnp.float32)
        for start in (first, pixels + first):
            span = slice(start, start + CHUNK)
            uv[:, span] = weight * jnp.dot(pick, particles(span), preferred_element_type=jnp.float32)
    penalty = penalty_ref[spots[0]] if have_penalty else penalties_of(views, dtab_ref, ori, pixels)
    pens[...] = jnp.dot(group_hot, jnp.concatenate(three(penalty), axis=0),
                        preferred_element_type=jnp.float32)
    label = label_ref[...]

    def one_tile(start, size):
        mine = pl.ds(pl.multiple_of(start, HALF), size)
        here = info[mine, :]
        hot = jnp.concatenate(
            [jnp.where(here[:, t:t + 1] == label, 1.0, 0.0) for t in range(trans)], axis=0
        ).astype(jnp.bfloat16)
        for first in range(0, pixels, PIECE):
            phase = jnp.dot(hot, table_ref[:, 2 * first:2 * (first + PIECE)],
                            preferred_element_type=jnp.float32)
            real = uv[mine, first:first + PIECE]
            imag = uv[mine, pixels + first:pixels + first + PIECE]
            for t in range(trans):
                rows = slice(t * size, (t + 1) * size)
                cosine = phase[rows, :PIECE]
                sine = phase[rows, PIECE:]
                shifted[rows, first:first + PIECE] = (real * cosine + imag * sine).astype(jnp.bfloat16)
                shifted[rows, pixels + first:pixels + first + PIECE] = (
                    imag * cosine - real * sine).astype(jnp.bfloat16)
        scores = lax.dot_general(shifted[:trans * size, :], views(slice(0, 2 * pixels)), contract_last,
                                 preferred_element_type=jnp.float32)
        full = scores.reshape(trans, size, ori) + pens[mine, :][None]
        highest = jnp.max(jnp.max(full, axis=0), axis=1, keepdims=True)
        total = jnp.zeros((size, ori), jnp.float32)
        moment_x = jnp.zeros((size, ori), jnp.float32)
        moment_y = jnp.zeros((size, ori), jnp.float32)
        for t in range(trans):
            term = jnp.exp(full[t] - highest)
            total += term
            moment_x += term * here[:, trans + 1 + t:trans + 2 + t]
            moment_y += term * here[:, 2 * trans + 1 + t:2 * trans + 2 + t]
        total = jnp.sum(total, axis=1, keepdims=True)
        moment_x = jnp.sum(moment_x, axis=1, keepdims=True)
        moment_y = jnp.sum(moment_y, axis=1, keepdims=True)
        lanes = lax.broadcasted_iota(jnp.int32, (size, 128), 1)
        stats[mine, :] = jnp.where(
            lanes == 0, highest,
            jnp.where(lanes == 1, total, jnp.where(lanes == 2, moment_x,
                                                   jnp.where(lanes == 3, moment_y, 0.0))))

    halves = tiles_ref[0]

    @pl.loop(0, halves // 2)
    def _(tile):
        one_tile(tile * TILE, TILE)

    @pl.when(halves % 2 == 1)
    def _():
        one_tile((halves - 1) * HALF, HALF)

    back = sum(
        lax.dot_general(part, pick, (((0,), (0,)), ((), ())), preferred_element_type=jnp.float32)
        for part in three(stats[...])
    )
    out_ref[0] = back[:8, :]


def class_stats(tiles, rank, meta, label, table, wtab, dtab, penalty, x_parts, q_parts, trans, slots):
    rows_all = rank.shape[1]
    rows_q, width = q_parts[0][0].shape[1:]
    ori = rows_q * len(q_parts)
    arrays = [array for array, _ in q_parts]
    spots = [spot for _, spot in q_parts]
    extra = [] if penalty is None else [penalty]
    vmem = pl.BlockSpec(memory_space=pltpu.VMEM)
    return pl.pallas_call(
        functools.partial(stats_kernel, trans, spots, len(x_parts), penalty is not None),
        out_shape=jax.ShapeDtypeStruct((1, 8, rows_all), jnp.float32),
        in_specs=[pl.BlockSpec(memory_space=pltpu.SMEM)]
        + [vmem] * (6 + len(extra) + len(x_parts) + len(arrays)),
        out_specs=vmem,
        scratch_shapes=[
            pltpu.VMEM((slots, width), jnp.float32),
            pltpu.VMEM((slots, ori), jnp.float32),
            pltpu.VMEM((slots, 128), jnp.float32),
            pltpu.VMEM((slots, 128), jnp.float32),
            pltpu.VMEM((trans * TILE, width), jnp.bfloat16),
        ],
        compiler_params=pltpu.CompilerParams(vmem_limit_bytes=36 * 1024 * 1024),
        cost_estimate=pl.CostEstimate(
            flops=20 * slots * trans * width * (ori + 256),
            bytes_accessed=(rows_all + ori) * width * 2,
            transcendentals=0,
        ),
    )(tiles, rank, meta, label, table, wtab, dtab, *extra, *x_parts, *arrays)


def on_device(particles, candidates, ctf_ids, offsets, ctf_table, sigma_sq, projections):
    pose_count = lax.axis_size("pose")
    dom_count = lax.axis_size("dom")
    pose = lax.axis_index("pose")
    local = projections.shape[0]
    class_total = local * pose_count
    rows, picks = candidates.shape
    trans = offsets.shape[2]
    pixels = sigma_sq.shape[0]
    capacity = 3 * rows * picks // class_total
    share = min(SHARE, pose_count)
    share_bits = [1 << b for b in range(share.bit_length() - 1)]
    families = pose_count // share
    slots = -(-min(share * capacity, share * rows) // TILE) * TILE

    dom_bits = [1 << b for b in range(dom_count.bit_length() - 1)][::-1]

    order = [0]
    for bit in share_bits[::-1]:
        order = order + [member ^ bit for member in order]

    single = {bit: swap(particles, "pose", bit) for bit in share_bits[::-1]}
    own_pieces = [projections] + [swap(projections, "dom", bit) for bit in dom_bits]
    chunks = [projections[spot:spot + 1] for spot in range(local)]

    offsets, *_ = lax.optimization_barrier((offsets, own_pieces[-1]))
    offset_f = offsets.astype(jnp.float32)
    combo = (offset_f[:, 0] + REACH) * (2 * REACH + 1) + (offset_f[:, 1] + REACH)
    meta = jnp.concatenate(
        [combo, ctf_ids[:, None].astype(jnp.float32), offset_f[:, 0], offset_f[:, 1],
         candidates.astype(jnp.float32)], axis=1)
    meta = jnp.pad(meta, ((0, 0), (0, 128 - meta.shape[1]))).astype(jnp.bfloat16)
    metas = [swap(meta, "pose", member) if member else meta for member in order]
    meta_all = jnp.concatenate(metas, axis=0)

    single, own_pieces, chunks = lax.optimization_barrier((single, own_pieces, chunks))

    x_parts = []
    for member in order:
        bits = [bit for bit in share_bits if member & bit]
        part = single[bits[-1]] if bits else particles
        for bit in bits[:-1]:
            part = swap(part, "pose", bit)
        x_parts.append(part)

    far = []
    for family in range(1, families):
        members = []
        for spot in range(local):
            if members:
                chunks[spot], members[-1] = lax.optimization_barrier((chunks[spot], members[-1]))
            members.append(swap(chunks[spot], "pose", family * share))
        far.append(members)
    own_pieces = own_pieces + [swap(own_pieces[1], "dom", bit) for bit in dom_bits[1:]]

    named = meta_all[:, 3 * trans + 1:3 * trans + 1 + picks].astype(jnp.int32)
    owner = pose ^ (jnp.arange(families, dtype=jnp.int32) * share)
    class_ids = (owner[:, None] * local + jnp.arange(local, dtype=jnp.int32)[None, :]).reshape(-1)
    names = jnp.any(named.T[None, :, :] == class_ids[:, None, None], axis=1).astype(jnp.int32)
    ahead = jnp.cumsum(names, axis=1)
    rank = jnp.where(names > 0, ahead - 1, -1)
    tiles = (ahead[:, -1] + (HALF - 1)) // HALF

    weight = ctf_table / sigma_sq[None, :]
    wtab = jnp.concatenate(split_three(weight), axis=0)
    dtab = jnp.concatenate(split_three(weight * ctf_table), axis=0)

    table, label = phase_table(pixels)
    table, label = jnp.asarray(table), jnp.asarray(label)
    own_penalty = own_penalties(dtab, own_pieces)
    results = []

    def one_class(index, members, penalty):
        turn = tiles[index:index + 1]
        if results:
            turn, results[-1] = lax.optimization_barrier((turn, results[-1]))
        results.append(class_stats(turn, rank[index:index + 1], meta_all, label, table, wtab, dtab, penalty,
                                   x_parts, members, trans, slots))

    for spot in range(local):
        one_class(spot, [(piece, spot) for piece in own_pieces], own_penalty)
    for family in range(1, families):
        for spot in range(local):
            pieces = [far[family - 1][spot]]
            for hop, bit in enumerate(dom_bits):
                if spot:
                    tie = -1 if hop else spot
                    pieces[hop:], results[tie] = lax.optimization_barrier((pieces[hop:], results[tie]))
                pieces = pieces + [swap(member, "dom", bit) for member in pieces]
            one_class(family * local + spot, [(member, 0) for member in pieces], None)
    stats = jnp.concatenate(results, axis=0)[:, :4, :]
    own = []
    for place, member in enumerate(order):
        block = stats[:, :, place * rows:(place + 1) * rows]
        block = swap(block, "pose", member) if member else block
        own += [(member, spot, block[spot]) for spot in range(families * local)]

    cand = candidates.T
    owner = cand // local
    beyond = (owner ^ pose) // share
    within = (owner ^ pose) % share
    position = beyond * local + cand % local
    picked = jnp.zeros((picks, 4, rows), jnp.float32)
    for member, spot, block in own:
        hit = (within == member) & (position == spot)
        picked = jnp.where(hit[:, None, :], block[None], picked)
    log_weight = picked[:, 0] + jnp.log(picked[:, 1])
    raw_weight = jnp.exp(log_weight - jnp.max(log_weight, axis=0, keepdims=True))
    class_prob = raw_weight / jnp.sum(raw_weight, axis=0, keepdims=True)
    mean_x = jnp.sum(class_prob * picked[:, 2] / picked[:, 1], axis=0)
    mean_y = jnp.sum(class_prob * picked[:, 3] / picked[:, 1], axis=0)
    return (class_prob.T, jnp.stack([mean_x, mean_y], axis=1))


def solution(mesh):
    in_specs = (
        P(("pose", "dom"), None),
        P(("pose", "dom"), None),
        P(("pose", "dom")),
        P(("pose", "dom"), None, None),
        P(),
        P(),
        P("pose", "dom", None),
    )
    out_specs = (P(("pose", "dom"), None), P(("pose", "dom"), None))
    return jax.shard_map(
        on_device, mesh=mesh, in_specs=in_specs, out_specs=out_specs, check_vma=False
    )
```

```python
import functools

import jax
import jax.numpy as jnp
import ml_dtypes
import numpy as np
from jax import lax
from jax.experimental import pallas as pl
from jax.experimental.pallas import tpu as pltpu
from jax.sharding import PartitionSpec as P

BOX = 128
GRID_X = 64
REACH = 3
SHARE = 4
TILE = 32
CHUNK = 512
PIECE = 256
HIGHEST = lax.Precision.HIGHEST


def split_three(values):
    parts = []
    for _ in range(3):
        part = lax.reduce_precision(values, 8, 7)
        parts.append(part.astype(jnp.bfloat16))
        values = values - part
    return parts


def phase_table(pixel_count):
    levels = np.arange(-REACH, REACH + 1)
    pixel = np.arange(pixel_count)
    shift_x = np.repeat(levels, levels.size)[:, None]
    shift_y = np.tile(levels, levels.size)[:, None]
    angle = 2.0 * np.pi / BOX * (shift_x * (pixel % GRID_X - 32) + shift_y * (pixel // GRID_X))
    rest = np.concatenate([np.cos(angle), np.sin(angle)], axis=1).astype(np.float32)
    parts = []
    for _ in range(3):
        part = rest.astype(ml_dtypes.bfloat16)
        parts.append(part)
        rest = rest - part.astype(np.float32)
    rows = np.concatenate(parts, axis=0)
    count = levels.size**2
    padded = np.zeros((256, 2 * pixel_count), ml_dtypes.bfloat16)
    padded[: rows.shape[0]] = rows
    label = np.full((1, 256), -1.0, np.float32)
    label[0, : rows.shape[0]] = np.arange(rows.shape[0]) % count
    return (padded, label)


def swap(values, axis, bit):
    count = lax.axis_size(axis)
    return lax.ppermute(values, axis, [(index, index ^ bit) for index in range(count)])


def three(values):
    high = values.astype(jnp.bfloat16)
    rest = values - high.astype(jnp.float32)
    middle = rest.astype(jnp.bfloat16)
    return [high, middle, (rest - middle.astype(jnp.float32)).astype(jnp.bfloat16)]


contract_last = (((1,), (1,)), ((), ()))


def penalties_of(views, dtab_ref, ori, pixels):
    groups = dtab_ref.shape[0] // 3
    parted = jnp.zeros((3 * groups, ori), jnp.float32)
    for first in range(0, pixels, CHUNK):
        real = views(slice(first, first + CHUNK)).astype(jnp.float32)
        imag = views(slice(pixels + first, pixels + first + CHUNK)).astype(jnp.float32)
        for part in three(real * real + imag * imag)[:2]:
            parted += lax.dot_general(dtab_ref[:, first:first + CHUNK], part, contract_last,
                                      preferred_element_type=jnp.float32)
    return -0.5 * (parted[:groups] + parted[groups:2 * groups] + parted[2 * groups:])


def views_of(q_refs, spots):
    def views(cols):
        return jnp.concatenate([member[spot, :, cols] for member, spot in zip(q_refs, spots)], axis=0)
    return views


def penalty_kernel(pieces, dtab_ref, *refs):
    out_ref = refs[pieces]
    for place in range(out_ref.shape[0]):
        views = views_of(refs[:pieces], [place] * pieces)
        out_ref[place] = penalties_of(views, dtab_ref, out_ref.shape[2], dtab_ref.shape[1])


def own_penalties(dtab, pieces):
    classes, rows_q, width = pieces[0].shape
    ori = rows_q * len(pieces)
    vmem = pl.BlockSpec(memory_space=pltpu.VMEM)
    return pl.pallas_call(
        functools.partial(penalty_kernel, len(pieces)),
        out_shape=jax.ShapeDtypeStruct((classes, dtab.shape[0] // 3, ori), jnp.float32),
        in_specs=[vmem] * (1 + len(pieces)),
        out_specs=vmem,
        compiler_params=pltpu.CompilerParams(vmem_limit_bytes=24 * 1024 * 1024),
    )(dtab, *pieces)


def stats_kernel(trans, index, spots, share, have_penalty, ids_ref, label_ref, table_ref, wtab_ref,
                 dtab_ref, *refs):
    if have_penalty:
        penalty_ref, refs = refs[0], refs[1:]
    meta_refs, refs = refs[:share], refs[share:]
    x_refs, refs = refs[:share], refs[share:]
    q_refs = refs[:len(spots)]
    out_ref, uv, pens, info, stats = refs[len(spots):]
    rows_all = out_ref.shape[2]
    slots = uv.shape[0]
    pixels = uv.shape[1] // 2
    ori = pens.shape[1]
    groups = dtab_ref.shape[0] // 3
    views = views_of(q_refs, spots)

    def particles(cols):
        return jnp.concatenate([member[:, cols] for member in x_refs], axis=0)

    meta = jnp.concatenate([member[...] for member in meta_refs], axis=1)
    named = meta[3 * trans + 1:, :].astype(jnp.float32)
    wanted = ids_ref[index].astype(jnp.float32)
    names = jnp.max(jnp.where(named == wanted, 1.0, 0.0), axis=0, keepdims=True)
    before = lax.broadcasted_iota(jnp.int32, (rows_all, rows_all), 0)
    after = lax.broadcasted_iota(jnp.int32, (rows_all, rows_all), 1)
    upper = jnp.where(before <= after, 1.0, 0.0).astype(jnp.bfloat16)
    ahead = jnp.dot(jnp.broadcast_to(names, (16, rows_all)).astype(jnp.bfloat16), upper,
                    preferred_element_type=jnp.float32)[:1]
    rank = jnp.where(names > 0.0, ahead - 1.0, -1.0).astype(jnp.int32)
    tiles = (jnp.max(ahead).astype(jnp.int32) + (TILE - 1)) // TILE

    row = lax.broadcasted_iota(jnp.int32, (slots, rows_all), 0)
    pick = jnp.where(rank == row, 1.0, 0.0).astype(jnp.bfloat16)
    info[...] = lax.dot_general(pick, meta, contract_last, preferred_element_type=jnp.float32)
    lane = lax.broadcasted_iota(jnp.int32, (slots, 3 * groups), 1)
    group_hot = jnp.where(info[:, trans:trans + 1] == (lane % groups).astype(jnp.float32), 1.0, 0.0)
    group_hot = group_hot.astype(jnp.bfloat16)
    stats[...] = jnp.zeros_like(stats)
    for first in range(0, pixels, CHUNK):
        weight = jnp.dot(group_hot, wtab_ref[:, first:first + CHUNK], preferred_element_type=jnp.float32)
        for start in (first, pixels + first):
            span = slice(start, start + CHUNK)
            uv[:, span] = weight * jnp.dot(pick, particles(span), preferred_element_type=jnp.float32)
    penalty = penalty_ref[spots[0]] if have_penalty else penalties_of(views, dtab_ref, ori, pixels)
    pens[...] = jnp.dot(group_hot, jnp.concatenate(three(penalty), axis=0),
                        preferred_element_type=jnp.float32)
    label = label_ref[...]

    @pl.loop(0, tiles)
    def _(tile):
        mine = pl.ds(pl.multiple_of(tile * TILE, TILE), TILE)
        here = info[mine, :]
        hot = jnp.concatenate(
            [jnp.where(here[:, t:t + 1] == label, 1.0, 0.0) for t in range(trans)], axis=0
        ).astype(jnp.bfloat16)
        scores = jnp.zeros((trans * TILE, ori), jnp.float32)
        for first in range(0, pixels, PIECE):
            cols = slice(first, first + PIECE)
            icols = slice(pixels + first, pixels + first + PIECE)
            cosine = jnp.dot(hot, table_ref[:, cols], preferred_element_type=jnp.float32)
            sine = jnp.dot(hot, table_ref[:, icols], preferred_element_type=jnp.float32)
            cosine = cosine.reshape(trans, TILE, PIECE)
            sine = sine.reshape(trans, TILE, PIECE)
            real = uv[mine, cols][None]
            imag = uv[mine, icols][None]
            shift_re = (real * cosine + imag * sine).astype(jnp.bfloat16)
            shift_im = (imag * cosine - real * sine).astype(jnp.bfloat16)
            scores += lax.dot_general(shift_re.reshape(trans * TILE, PIECE), views(cols), contract_last,
                                      preferred_element_type=jnp.float32)
            scores += lax.dot_general(shift_im.reshape(trans * TILE, PIECE), views(icols), contract_last,
                                      preferred_element_type=jnp.float32)
        full = scores.reshape(trans, TILE, ori) + pens[mine, :][None]
        highest = jnp.max(jnp.max(full, axis=0), axis=1, keepdims=True)
        total = jnp.zeros((TILE, ori), jnp.float32)
        moment_x = jnp.zeros((TILE, ori), jnp.float32)
        moment_y = jnp.zeros((TILE, ori), jnp.float32)
        for t in range(trans):
            term = jnp.exp(full[t] - highest)
            total += term
            moment_x += term * here[:, trans + 1 + t:trans + 2 + t]
            moment_y += term * here[:, 2 * trans + 1 + t:2 * trans + 2 + t]
        total = jnp.sum(total, axis=1, keepdims=True)
        moment_x = jnp.sum(moment_x, axis=1, keepdims=True)
        moment_y = jnp.sum(moment_y, axis=1, keepdims=True)
        lanes = lax.broadcasted_iota(jnp.int32, (TILE, 128), 1)
        stats[mine, :] = jnp.where(
            lanes == 0, highest,
            jnp.where(lanes == 1, total, jnp.where(lanes == 2, moment_x,
                                                   jnp.where(lanes == 3, moment_y, 0.0))))

    back = sum(
        lax.dot_general(part, pick, (((0,), (0,)), ((), ())), preferred_element_type=jnp.float32)
        for part in three(stats[...])
    )
    out_ref[0] = back[:8, :]


def class_stats(index, ids, label, table, wtab, dtab, penalty, metas, x_parts, q_parts, trans, slots):
    rows_all = sum(part.shape[0] for part in x_parts)
    rows_q, width = q_parts[0][0].shape[1:]
    ori = rows_q * len(q_parts)
    arrays = [array for array, _ in q_parts]
    spots = [spot for _, spot in q_parts]
    extra = [] if penalty is None else [penalty]
    vmem = pl.BlockSpec(memory_space=pltpu.VMEM)
    return pl.pallas_call(
        functools.partial(stats_kernel, trans, index, spots, len(x_parts), penalty is not None),
        out_shape=jax.ShapeDtypeStruct((1, 8, rows_all), jnp.float32),
        in_specs=[pl.BlockSpec(memory_space=pltpu.SMEM)]
        + [vmem] * (4 + len(extra) + 2 * len(x_parts) + len(arrays)),
        out_specs=vmem,
        scratch_shapes=[
            pltpu.VMEM((slots, width), jnp.float32),
            pltpu.VMEM((slots, ori), jnp.float32),
            pltpu.VMEM((slots, metas[0].shape[0]), jnp.float32),
            pltpu.VMEM((slots, 128), jnp.float32),
        ],
        compiler_params=pltpu.CompilerParams(vmem_limit_bytes=28 * 1024 * 1024),
        cost_estimate=pl.CostEstimate(
            flops=20 * slots * trans * width * (ori + 256),
            bytes_accessed=(rows_all + ori) * width * 2,
            transcendentals=0,
        ),
    )(ids, label, table, wtab, dtab, *extra, *metas, *x_parts, *arrays)


def on_device(particles, candidates, ctf_ids, offsets, ctf_table, sigma_sq, projections):
    pose_count = lax.axis_size("pose")
    dom_count = lax.axis_size("dom")
    pose = lax.axis_index("pose")
    local = projections.shape[0]
    class_total = local * pose_count
    rows, picks = candidates.shape
    trans = offsets.shape[2]
    pixels = sigma_sq.shape[0]
    capacity = 3 * rows * picks // class_total
    share = min(SHARE, pose_count)
    share_bits = [1 << b for b in range(share.bit_length() - 1)]
    families = pose_count // share

    def slots_for(blocks):
        return -(-min(blocks * capacity, blocks * rows) // TILE) * TILE

    dom_bits = [1 << b for b in range(dom_count.bit_length() - 1)][::-1]

    order = [0]
    for bit in share_bits[::-1]:
        order = order + [member ^ bit for member in order]

    near = len([member for member in order if bin(member).count("1") < 2])

    single = {bit: swap(particles, "pose", bit) for bit in share_bits[::-1]}
    own_pieces = [projections] + [swap(projections, "dom", bit) for bit in dom_bits]
    chunks = [projections[spot:spot + 1] for spot in range(local)]
    far = [[swap(chunks[0], "pose", family * share)] for family in range(1, families)]

    offsets, *_ = lax.optimization_barrier((offsets, own_pieces[-1]))
    offset_t = offsets.transpose(1, 2, 0).astype(jnp.float32)
    combo = (offset_t[0] + REACH) * (2 * REACH + 1) + (offset_t[1] + REACH)
    meta = jnp.concatenate(
        [combo, ctf_ids[None, :].astype(jnp.float32), offset_t[0], offset_t[1],
         candidates.T.astype(jnp.float32)], axis=0)
    meta = jnp.pad(meta, ((0, -meta.shape[0] % 16), (0, 0)), constant_values=-1.0).astype(jnp.bfloat16)
    metas = [swap(meta, "pose", member) if member else meta for member in order]

    single, own_pieces, chunks, far = lax.optimization_barrier((single, own_pieces, chunks, far))

    x_parts = []
    for member in order:
        bits = [bit for bit in share_bits if member & bit]
        part = single[bits[-1]] if bits else particles
        for bit in bits[:-1]:
            part = swap(part, "pose", bit)
        x_parts.append(part)
    for family in range(1, families):
        far[family - 1] += [swap(chunk, "pose", family * share) for chunk in chunks[1:]]
    own_pieces = own_pieces + [swap(own_pieces[1], "dom", bit) for bit in dom_bits[1:]]

    weight = ctf_table / sigma_sq[None, :]
    wtab = jnp.concatenate(split_three(weight), axis=0)
    dtab = jnp.concatenate(split_three(weight * ctf_table), axis=0)
    own_penalty = own_penalties(dtab, own_pieces)
    owner = pose ^ (jnp.arange(families, dtype=jnp.int32) * share)
    ids = (owner[:, None] * local + jnp.arange(local, dtype=jnp.int32)[None, :]).reshape(-1)
    table, label = phase_table(pixels)
    table, label = jnp.asarray(table), jnp.asarray(label)
    results = {}
    latest = []

    def one_class(index, members, penalty, first, last):
        turn = ids
        if latest:
            turn, results[latest[-1]] = lax.optimization_barrier((turn, results[latest[-1]]))
        results[(index, first)] = class_stats(
            index, turn, label, table, wtab, dtab, penalty, metas[first:last], x_parts[first:last], members,
            trans, slots_for(last - first))
        latest.append((index, first))

    own = [[(piece, spot) for piece in own_pieces] for spot in range(local)]
    for spot in range(local):
        one_class(spot, own[spot], own_penalty, 0, near)
    for family in range(1, families):
        for spot in range(local):
            pieces = [far[family - 1][spot]]
            for hop, bit in enumerate(dom_bits):
                if spot:
                    key = latest[-1] if hop else (spot, 0)
                    pieces[hop:], results[key] = lax.optimization_barrier((pieces[hop:], results[key]))
                pieces = pieces + [swap(member, "dom", bit) for member in pieces]
            one_class(family * local + spot, [(member, 0) for member in pieces], None, 0, share)
            if family == 1 and near < share:
                one_class(spot, own[spot], own_penalty, near, share)

    own = []
    for place, member in enumerate(order):
        block = []
        for spot in range(families * local):
            first = near if spot < local and place >= near else 0
            start = (place - first) * rows
            block.append(results[(spot, first)][:, :4, start:start + rows])
        block = jnp.concatenate(block, axis=0)
        block = swap(block, "pose", member) if member else block
        own += [(member, spot, block[spot]) for spot in range(families * local)]

    cand = candidates.T
    owner = cand // local
    beyond = (owner ^ pose) // share
    within = (owner ^ pose) % share
    position = beyond * local + cand % local
    picked = jnp.zeros((picks, 4, rows), jnp.float32)
    for member, spot, block in own:
        hit = (within == member) & (position == spot)
        picked = jnp.where(hit[:, None, :], block[None], picked)
    log_weight = picked[:, 0] + jnp.log(picked[:, 1])
    raw_weight = jnp.exp(log_weight - jnp.max(log_weight, axis=0, keepdims=True))
    class_prob = raw_weight / jnp.sum(raw_weight, axis=0, keepdims=True)
    mean_x = jnp.sum(class_prob * picked[:, 2] / picked[:, 1], axis=0)
    mean_y = jnp.sum(class_prob * picked[:, 3] / picked[:, 1], axis=0)
    return (class_prob.T, jnp.stack([mean_x, mean_y], axis=1))


def solution(mesh):
    in_specs = (
        P(("pose", "dom"), None),
        P(("pose", "dom"), None),
        P(("pose", "dom")),
        P(("pose", "dom"), None, None),
        P(),
        P(),
        P("pose", "dom", None),
    )
    out_specs = (P(("pose", "dom"), None), P(("pose", "dom"), None))
    return jax.shard_map(
        on_device, mesh=mesh, in_specs=in_specs, out_specs=out_specs, check_vma=False
    )
```

```python
import functools

import jax
import jax.numpy as jnp
import ml_dtypes
import numpy as np
from jax import lax
from jax.experimental import pallas as pl
from jax.experimental.pallas import tpu as pltpu
from jax.sharding import PartitionSpec as P

BOX = 128
GRID_X = 64
REACH = 3
SHARE = 4
TILE = 32
CHUNK = 512
PIECE = 256
HIGHEST = lax.Precision.HIGHEST


def split_three(values):
    parts = []
    for _ in range(3):
        part = lax.reduce_precision(values, 8, 7)
        parts.append(part.astype(jnp.bfloat16))
        values = values - part
    return parts


def phase_table(pixel_count):
    levels = np.arange(-REACH, REACH + 1)
    pixel = np.arange(pixel_count)
    shift_x = np.repeat(levels, levels.size)[:, None]
    shift_y = np.tile(levels, levels.size)[:, None]
    angle = 2.0 * np.pi / BOX * (shift_x * (pixel % GRID_X - 32) + shift_y * (pixel // GRID_X))
    rest = np.concatenate([np.cos(angle), np.sin(angle)], axis=1).astype(np.float32)
    parts = []
    for _ in range(3):
        part = rest.astype(ml_dtypes.bfloat16)
        parts.append(part)
        rest = rest - part.astype(np.float32)
    rows = np.concatenate(parts, axis=0)
    count = levels.size**2
    padded = np.zeros((256, 2 * pixel_count), ml_dtypes.bfloat16)
    padded[: rows.shape[0]] = rows
    label = np.full((1, 256), -1.0, np.float32)
    label[0, : rows.shape[0]] = np.arange(rows.shape[0]) % count
    return (padded, label)


def swap(values, axis, bit):
    count = lax.axis_size(axis)
    return lax.ppermute(values, axis, [(index, index ^ bit) for index in range(count)])


def three(values):
    high = values.astype(jnp.bfloat16)
    rest = values - high.astype(jnp.float32)
    middle = rest.astype(jnp.bfloat16)
    return [high, middle, (rest - middle.astype(jnp.float32)).astype(jnp.bfloat16)]


contract_last = (((1,), (1,)), ((), ()))


def penalties_of(views, dtab_ref, ori, pixels):
    groups = dtab_ref.shape[0] // 3
    parted = jnp.zeros((3 * groups, ori), jnp.float32)
    for first in range(0, pixels, CHUNK):
        real = views(slice(first, first + CHUNK)).astype(jnp.float32)
        imag = views(slice(pixels + first, pixels + first + CHUNK)).astype(jnp.float32)
        for part in three(real * real + imag * imag)[:2]:
            parted += lax.dot_general(dtab_ref[:, first:first + CHUNK], part, contract_last,
                                      preferred_element_type=jnp.float32)
    return -0.5 * (parted[:groups] + parted[groups:2 * groups] + parted[2 * groups:])


def views_of(q_refs, spots):
    def views(cols):
        return jnp.concatenate([member[spot, :, cols] for member, spot in zip(q_refs, spots)], axis=0)
    return views


def penalty_kernel(pieces, dtab_ref, *refs):
    out_ref = refs[pieces]
    for place in range(out_ref.shape[0]):
        views = views_of(refs[:pieces], [place] * pieces)
        out_ref[place] = penalties_of(views, dtab_ref, out_ref.shape[2], dtab_ref.shape[1])


def own_penalties(dtab, pieces):
    classes, rows_q, width = pieces[0].shape
    ori = rows_q * len(pieces)
    vmem = pl.BlockSpec(memory_space=pltpu.VMEM)
    return pl.pallas_call(
        functools.partial(penalty_kernel, len(pieces)),
        out_shape=jax.ShapeDtypeStruct((classes, dtab.shape[0] // 3, ori), jnp.float32),
        in_specs=[vmem] * (1 + len(pieces)),
        out_specs=vmem,
        compiler_params=pltpu.CompilerParams(vmem_limit_bytes=24 * 1024 * 1024),
    )(dtab, *pieces)


def stats_kernel(trans, index, spots, share, have_penalty, ids_ref, label_ref, table_ref, wtab_ref,
                 dtab_ref, *refs):
    if have_penalty:
        penalty_ref, refs = refs[0], refs[1:]
    x_refs, refs = refs[:share], refs[share:]
    q_refs = refs[:len(spots)]
    out_ref, uv, pens, info, stats = refs[len(spots):]
    rows_all = out_ref.shape[2]
    rows = rows_all // share
    features = info.shape[1]
    slots = uv.shape[0]
    pixels = uv.shape[1] // 2
    ori = pens.shape[1]
    groups = dtab_ref.shape[0] // 3
    views = views_of(q_refs, spots)

    def particles(cols):
        return jnp.concatenate([member[:rows, cols] for member in x_refs], axis=0)

    below = [member[rows:rows + 8, :features // 8 * rows].astype(jnp.float32) for member in x_refs]
    meta = jnp.concatenate(
        [jnp.concatenate([block[:, at * rows:(at + 1) * rows] for at in range(features // 8)], axis=0)
         for block in below], axis=1)
    named = meta[3 * trans + 1:, :]
    meta = meta.astype(jnp.bfloat16)
    wanted = ids_ref[index].astype(jnp.float32)
    names = jnp.max(jnp.where(named == wanted, 1.0, 0.0), axis=0, keepdims=True)
    before = lax.broadcasted_iota(jnp.int32, (rows_all, rows_all), 0)
    after = lax.broadcasted_iota(jnp.int32, (rows_all, rows_all), 1)
    upper = jnp.where(before <= after, 1.0, 0.0).astype(jnp.bfloat16)
    ahead = jnp.dot(jnp.broadcast_to(names, (16, rows_all)).astype(jnp.bfloat16), upper,
                    preferred_element_type=jnp.float32)[:1]
    rank = jnp.where(names > 0.0, ahead - 1.0, -1.0).astype(jnp.int32)
    tiles = (jnp.max(ahead).astype(jnp.int32) + (TILE - 1)) // TILE

    row = lax.broadcasted_iota(jnp.int32, (slots, rows_all), 0)
    pick = jnp.where(rank == row, 1.0, 0.0).astype(jnp.bfloat16)
    info[...] = lax.dot_general(pick, meta, contract_last, preferred_element_type=jnp.float32)
    lane = lax.broadcasted_iota(jnp.int32, (slots, 3 * groups), 1)
    group_hot = jnp.where(info[:, trans:trans + 1] == (lane % groups).astype(jnp.float32), 1.0, 0.0)
    group_hot = group_hot.astype(jnp.bfloat16)
    stats[...] = jnp.zeros_like(stats)
    for first in range(0, pixels, CHUNK):
        weight = jnp.dot(group_hot, wtab_ref[:, first:first + CHUNK], preferred_element_type=jnp.float32)
        for start in (first, pixels + first):
            span = slice(start, start + CHUNK)
            uv[:, span] = weight * jnp.dot(pick, particles(span), preferred_element_type=jnp.float32)
    penalty = penalty_ref[spots[0]] if have_penalty else penalties_of(views, dtab_ref, ori, pixels)
    pens[...] = jnp.dot(group_hot, jnp.concatenate(three(penalty), axis=0),
                        preferred_element_type=jnp.float32)
    label = label_ref[...]

    @pl.loop(0, tiles)
    def _(tile):
        mine = pl.ds(pl.multiple_of(tile * TILE, TILE), TILE)
        here = info[mine, :]
        hot = jnp.concatenate(
            [jnp.where(here[:, t:t + 1] == label, 1.0, 0.0) for t in range(trans)], axis=0
        ).astype(jnp.bfloat16)
        scores = jnp.zeros((trans * TILE, ori), jnp.float32)
        for first in range(0, pixels, PIECE):
            cols = slice(first, first + PIECE)
            icols = slice(pixels + first, pixels + first + PIECE)
            cosine = jnp.dot(hot, table_ref[:, cols], preferred_element_type=jnp.float32)
            sine = jnp.dot(hot, table_ref[:, icols], preferred_element_type=jnp.float32)
            cosine = cosine.reshape(trans, TILE, PIECE)
            sine = sine.reshape(trans, TILE, PIECE)
            real = uv[mine, cols][None]
            imag = uv[mine, icols][None]
            shift_re = (real * cosine + imag * sine).astype(jnp.bfloat16)
            shift_im = (imag * cosine - real * sine).astype(jnp.bfloat16)
            scores += lax.dot_general(shift_re.reshape(trans * TILE, PIECE), views(cols), contract_last,
                                      preferred_element_type=jnp.float32)
            scores += lax.dot_general(shift_im.reshape(trans * TILE, PIECE), views(icols), contract_last,
                                      preferred_element_type=jnp.float32)
        full = scores.reshape(trans, TILE, ori) + pens[mine, :][None]
        highest = jnp.max(jnp.max(full, axis=0), axis=1, keepdims=True)
        total = jnp.zeros((TILE, ori), jnp.float32)
        moment_x = jnp.zeros((TILE, ori), jnp.float32)
        moment_y = jnp.zeros((TILE, ori), jnp.float32)
        for t in range(trans):
            term = jnp.exp(full[t] - highest)
            total += term
            moment_x += term * here[:, trans + 1 + t:trans + 2 + t]
            moment_y += term * here[:, 2 * trans + 1 + t:2 * trans + 2 + t]
        total = jnp.sum(total, axis=1, keepdims=True)
        moment_x = jnp.sum(moment_x, axis=1, keepdims=True)
        moment_y = jnp.sum(moment_y, axis=1, keepdims=True)
        lanes = lax.broadcasted_iota(jnp.int32, (TILE, 128), 1)
        stats[mine, :] = jnp.where(
            lanes == 0, highest,
            jnp.where(lanes == 1, total, jnp.where(lanes == 2, moment_x,
                                                   jnp.where(lanes == 3, moment_y, 0.0))))

    back = sum(
        lax.dot_general(part, pick, (((0,), (0,)), ((), ())), preferred_element_type=jnp.float32)
        for part in three(stats[...])
    )
    out_ref[0] = back[:8, :]


def class_stats(index, ids, label, table, wtab, dtab, penalty, x_parts, q_parts, trans, slots, features):
    rows_all = sum(part.shape[0] - 8 for part in x_parts)
    rows_q, width = q_parts[0][0].shape[1:]
    ori = rows_q * len(q_parts)
    arrays = [array for array, _ in q_parts]
    spots = [spot for _, spot in q_parts]
    extra = [] if penalty is None else [penalty]
    vmem = pl.BlockSpec(memory_space=pltpu.VMEM)
    return pl.pallas_call(
        functools.partial(stats_kernel, trans, index, spots, len(x_parts), penalty is not None),
        out_shape=jax.ShapeDtypeStruct((1, 8, rows_all), jnp.float32),
        in_specs=[pl.BlockSpec(memory_space=pltpu.SMEM)]
        + [vmem] * (4 + len(extra) + len(x_parts) + len(arrays)),
        out_specs=vmem,
        scratch_shapes=[
            pltpu.VMEM((slots, width), jnp.float32),
            pltpu.VMEM((slots, ori), jnp.float32),
            pltpu.VMEM((slots, features), jnp.float32),
            pltpu.VMEM((slots, 128), jnp.float32),
        ],
        compiler_params=pltpu.CompilerParams(vmem_limit_bytes=28 * 1024 * 1024),
        cost_estimate=pl.CostEstimate(
            flops=20 * slots * trans * width * (ori + 256),
            bytes_accessed=(rows_all + ori) * width * 2,
            transcendentals=0,
        ),
    )(ids, label, table, wtab, dtab, *extra, *x_parts, *arrays)


def on_device(particles, candidates, ctf_ids, offsets, ctf_table, sigma_sq, projections):
    pose_count = lax.axis_size("pose")
    dom_count = lax.axis_size("dom")
    pose = lax.axis_index("pose")
    local = projections.shape[0]
    class_total = local * pose_count
    rows, picks = candidates.shape
    trans = offsets.shape[2]
    pixels = sigma_sq.shape[0]
    capacity = 3 * rows * picks // class_total
    share = min(SHARE, pose_count)
    share_bits = [1 << b for b in range(share.bit_length() - 1)]
    families = pose_count // share

    def slots_for(blocks):
        return -(-min(blocks * capacity, blocks * rows) // TILE) * TILE

    dom_bits = [1 << b for b in range(dom_count.bit_length() - 1)][::-1]

    order = [0]
    for bit in share_bits[::-1]:
        order = order + [member ^ bit for member in order]

    near = len([member for member in order if bin(member).count("1") < 2])

    offset_t = offsets.transpose(1, 2, 0).astype(jnp.float32)
    combo = (offset_t[0] + REACH) * (2 * REACH + 1) + (offset_t[1] + REACH)
    meta = jnp.concatenate(
        [combo, ctf_ids[None, :].astype(jnp.float32), offset_t[0], offset_t[1],
         candidates.T.astype(jnp.float32)], axis=0)
    features = -(-meta.shape[0] // 16) * 16
    meta = jnp.pad(meta, ((0, features - meta.shape[0]), (0, 0)), constant_values=-1.0)
    meta = meta.reshape(features // 8, 8, rows).transpose(1, 0, 2).reshape(8, -1).astype(jnp.bfloat16)
    meta = jnp.pad(meta, ((0, 0), (0, particles.shape[1] - meta.shape[1])))
    block = jnp.concatenate([particles, meta], axis=0)

    single = {bit: swap(block, "pose", bit) for bit in share_bits[::-1]}
    own_pieces = [projections] + [swap(projections, "dom", bit) for bit in dom_bits]
    own_pieces = own_pieces + [swap(own_pieces[1], "dom", bit) for bit in dom_bits[1:]]
    chunks = [projections[spot:spot + 1] for spot in range(local)]
    far = [[swap(chunks[0], "pose", family * share)] for family in range(1, families)]
    weight = ctf_table / sigma_sq[None, :]
    wtab = jnp.concatenate(split_three(weight), axis=0)
    dtab = jnp.concatenate(split_three(weight * ctf_table), axis=0)
    own_penalty = own_penalties(dtab, own_pieces)

    owner = pose ^ (jnp.arange(families, dtype=jnp.int32) * share)
    ids = (owner[:, None] * local + jnp.arange(local, dtype=jnp.int32)[None, :]).reshape(-1)
    single, chunks, far, own_penalty, ids = lax.optimization_barrier(
        (single, chunks, far, own_penalty, ids))

    x_parts = []
    for member in order:
        bits = [bit for bit in share_bits if member & bit]
        part = single[bits[-1]] if bits else block
        for bit in bits[:-1]:
            part = swap(part, "pose", bit)
        x_parts.append(part)
    for family in range(1, families):
        far[family - 1] += [swap(chunk, "pose", family * share) for chunk in chunks[1:]]
    table, label = phase_table(pixels)
    table, label = jnp.asarray(table), jnp.asarray(label)
    results = {}
    latest = []

    def one_class(index, members, penalty, first, last):
        turn = ids
        if latest:
            turn, results[latest[-1]] = lax.optimization_barrier((turn, results[latest[-1]]))
        results[(index, first)] = class_stats(
            index, turn, label, table, wtab, dtab, penalty, x_parts[first:last], members, trans,
            slots_for(last - first), features)
        latest.append((index, first))

    own = [[(piece, spot) for piece in own_pieces] for spot in range(local)]
    for spot in range(local):
        one_class(spot, own[spot], own_penalty, 0, near)
    for family in range(1, families):
        for spot in range(local):
            pieces = [far[family - 1][spot]]
            for hop, bit in enumerate(dom_bits):
                if spot or hop:
                    key = (family * local + spot - 1, 0) if hop and spot else (local - 1, 0)
                    pieces[hop:], results[key] = lax.optimization_barrier((pieces[hop:], results[key]))
                pieces = pieces + [swap(member, "dom", bit) for member in pieces]
            one_class(family * local + spot, [(member, 0) for member in pieces], None, 0, share)
            if family == 1 and spot == 0 and near < share:
                for place in range(local):
                    one_class(place, own[place], own_penalty, near, share)

    results = dict(zip(results, lax.optimization_barrier(tuple(results.values()))))
    own = []
    for place, member in enumerate(order):
        block = []
        for spot in range(families * local):
            first = near if spot < local and place >= near else 0
            start = (place - first) * rows
            block.append(results[(spot, first)][:, :4, start:start + rows])
        block = jnp.concatenate(block, axis=0)
        block = swap(block, "pose", member) if member else block
        own += [(member, spot, block[spot]) for spot in range(families * local)]

    cand = candidates.T
    owner = cand // local
    beyond = (owner ^ pose) // share
    within = (owner ^ pose) % share
    position = beyond * local + cand % local
    picked = jnp.zeros((picks, 4, rows), jnp.float32)
    for member, spot, block in own:
        hit = (within == member) & (position == spot)
        picked = jnp.where(hit[:, None, :], block[None], picked)
    log_weight = picked[:, 0] + jnp.log(picked[:, 1])
    raw_weight = jnp.exp(log_weight - jnp.max(log_weight, axis=0, keepdims=True))
    class_prob = raw_weight / jnp.sum(raw_weight, axis=0, keepdims=True)
    mean_x = jnp.sum(class_prob * picked[:, 2] / picked[:, 1], axis=0)
    mean_y = jnp.sum(class_prob * picked[:, 3] / picked[:, 1], axis=0)
    return (class_prob.T, jnp.stack([mean_x, mean_y], axis=1))


def solution(mesh):
    in_specs = (
        P(("pose", "dom"), None),
        P(("pose", "dom"), None),
        P(("pose", "dom")),
        P(("pose", "dom"), None, None),
        P(),
        P(),
        P("pose", "dom", None),
    )
    out_specs = (P(("pose", "dom"), None), P(("pose", "dom"), None))
    return jax.shard_map(
        on_device, mesh=mesh, in_specs=in_specs, out_specs=out_specs, check_vma=False
    )
```

```python
import functools

import jax
import jax.numpy as jnp
import ml_dtypes
import numpy as np
from jax import lax
from jax.experimental import pallas as pl
from jax.experimental.pallas import tpu as pltpu
from jax.sharding import PartitionSpec as P

BOX = 128
GRID_X = 64
REACH = 3
SHARE = 4
TILE = 32
CHUNK = 512
PIECE = 256
HIGHEST = lax.Precision.HIGHEST


def split_three(values):
    parts = []
    for _ in range(3):
        part = lax.reduce_precision(values, 8, 7)
        parts.append(part.astype(jnp.bfloat16))
        values = values - part
    return parts


def phase_table(pixel_count):
    levels = np.arange(-REACH, REACH + 1)
    pixel = np.arange(pixel_count)
    shift_x = np.repeat(levels, levels.size)[:, None]
    shift_y = np.tile(levels, levels.size)[:, None]
    angle = 2.0 * np.pi / BOX * (shift_x * (pixel % GRID_X - 32) + shift_y * (pixel // GRID_X))
    rest = np.concatenate([np.cos(angle), np.sin(angle)], axis=1).astype(np.float32)
    parts = []
    for _ in range(3):
        part = rest.astype(ml_dtypes.bfloat16)
        parts.append(part)
        rest = rest - part.astype(np.float32)
    rows = np.concatenate(parts, axis=0)
    count = levels.size**2
    padded = np.zeros((256, 2 * pixel_count), ml_dtypes.bfloat16)
    padded[: rows.shape[0]] = rows
    label = np.full((1, 256), -1.0, np.float32)
    label[0, : rows.shape[0]] = np.arange(rows.shape[0]) % count
    return (padded, label)


def swap(values, axis, bit):
    count = lax.axis_size(axis)
    return lax.ppermute(values, axis, [(index, index ^ bit) for index in range(count)])


def three(values):
    high = values.astype(jnp.bfloat16)
    rest = values - high.astype(jnp.float32)
    middle = rest.astype(jnp.bfloat16)
    return [high, middle, (rest - middle.astype(jnp.float32)).astype(jnp.bfloat16)]


contract_last = (((1,), (1,)), ((), ()))


def penalties_of(views, dtab_ref, ori, pixels):
    groups = dtab_ref.shape[0] // 3
    parted = jnp.zeros((3 * groups, ori), jnp.float32)
    for first in range(0, pixels, CHUNK):
        real = views(slice(first, first + CHUNK)).astype(jnp.float32)
        imag = views(slice(pixels + first, pixels + first + CHUNK)).astype(jnp.float32)
        for part in three(real * real + imag * imag)[:2]:
            parted += lax.dot_general(dtab_ref[:, first:first + CHUNK], part, contract_last,
                                      preferred_element_type=jnp.float32)
    return -0.5 * (parted[:groups] + parted[groups:2 * groups] + parted[2 * groups:])


def views_of(q_refs, spots):
    def views(cols):
        return jnp.concatenate([member[spot, :, cols] for member, spot in zip(q_refs, spots)], axis=0)
    return views


def penalty_kernel(pieces, dtab_ref, *refs):
    out_ref = refs[pieces]
    for place in range(out_ref.shape[0]):
        views = views_of(refs[:pieces], [place] * pieces)
        out_ref[place] = penalties_of(views, dtab_ref, out_ref.shape[2], dtab_ref.shape[1])


def own_penalties(dtab, pieces):
    classes, rows_q, width = pieces[0].shape
    ori = rows_q * len(pieces)
    vmem = pl.BlockSpec(memory_space=pltpu.VMEM)
    return pl.pallas_call(
        functools.partial(penalty_kernel, len(pieces)),
        out_shape=jax.ShapeDtypeStruct((classes, dtab.shape[0] // 3, ori), jnp.float32),
        in_specs=[vmem] * (1 + len(pieces)),
        out_specs=vmem,
        compiler_params=pltpu.CompilerParams(vmem_limit_bytes=24 * 1024 * 1024),
    )(dtab, *pieces)


def stats_kernel(trans, jobs, pieces, share, have_penalty, ids_ref, label_ref, table_ref, wtab_ref,
                 dtab_ref, *refs):
    if have_penalty:
        penalty_ref, refs = refs[0], refs[1:]
    x_refs, refs = refs[:share], refs[share:]
    q_refs = refs[:pieces]
    out_ref, uv, pens, info, stats = refs[pieces:]
    rows_all = out_ref.shape[2]
    rows = rows_all // share
    features = info.shape[1]
    slots = uv.shape[0]
    pixels = uv.shape[1] // 2
    ori = pens.shape[1]
    groups = dtab_ref.shape[0] // 3

    def particles(cols):
        return jnp.concatenate([member[:rows, cols] for member in x_refs], axis=0)

    below = [member[rows:rows + 8, :features // 8 * rows].astype(jnp.float32) for member in x_refs]
    meta = jnp.concatenate(
        [jnp.concatenate([block[:, at * rows:(at + 1) * rows] for at in range(features // 8)], axis=0)
         for block in below], axis=1)
    named = meta[3 * trans + 1:, :]
    meta = meta.astype(jnp.bfloat16)
    before = lax.broadcasted_iota(jnp.int32, (rows_all, rows_all), 0)
    after = lax.broadcasted_iota(jnp.int32, (rows_all, rows_all), 1)
    upper = jnp.where(before <= after, 1.0, 0.0).astype(jnp.bfloat16)
    label = label_ref[...]

    for place, (index, spot) in enumerate(jobs):
        views = views_of(q_refs, [spot] * pieces)
        wanted = ids_ref[index].astype(jnp.float32)
        names = jnp.max(jnp.where(named == wanted, 1.0, 0.0), axis=0, keepdims=True)
        ahead = jnp.dot(jnp.broadcast_to(names, (16, rows_all)).astype(jnp.bfloat16), upper,
                        preferred_element_type=jnp.float32)[:1]
        rank = jnp.where(names > 0.0, ahead - 1.0, -1.0).astype(jnp.int32)
        tiles = (jnp.max(ahead).astype(jnp.int32) + (TILE - 1)) // TILE

        row = lax.broadcasted_iota(jnp.int32, (slots, rows_all), 0)
        pick = jnp.where(rank == row, 1.0, 0.0).astype(jnp.bfloat16)
        info[...] = lax.dot_general(pick, meta, contract_last, preferred_element_type=jnp.float32)
        lane = lax.broadcasted_iota(jnp.int32, (slots, 3 * groups), 1)
        group_hot = jnp.where(info[:, trans:trans + 1] == (lane % groups).astype(jnp.float32), 1.0, 0.0)
        group_hot = group_hot.astype(jnp.bfloat16)
        stats[...] = jnp.zeros_like(stats)
        for first in range(0, pixels, CHUNK):
            weight = jnp.dot(group_hot, wtab_ref[:, first:first + CHUNK], preferred_element_type=jnp.float32)
            for start in (first, pixels + first):
                span = slice(start, start + CHUNK)
                uv[:, span] = weight * jnp.dot(pick, particles(span), preferred_element_type=jnp.float32)
        penalty = penalty_ref[spot] if have_penalty else penalties_of(views, dtab_ref, ori, pixels)
        pens[...] = jnp.dot(group_hot, jnp.concatenate(three(penalty), axis=0),
                            preferred_element_type=jnp.float32)

        @pl.loop(0, tiles)
        def _(tile):
            mine = pl.ds(pl.multiple_of(tile * TILE, TILE), TILE)
            here = info[mine, :]
            hot = jnp.concatenate(
                [jnp.where(here[:, t:t + 1] == label, 1.0, 0.0) for t in range(trans)], axis=0
            ).astype(jnp.bfloat16)
            scores = jnp.zeros((trans * TILE, ori), jnp.float32)
            for first in range(0, pixels, PIECE):
                cols = slice(first, first + PIECE)
                icols = slice(pixels + first, pixels + first + PIECE)
                cosine = jnp.dot(hot, table_ref[:, cols], preferred_element_type=jnp.float32)
                sine = jnp.dot(hot, table_ref[:, icols], preferred_element_type=jnp.float32)
                cosine = cosine.reshape(trans, TILE, PIECE)
                sine = sine.reshape(trans, TILE, PIECE)
                real = uv[mine, cols][None]
                imag = uv[mine, icols][None]
                shift_re = (real * cosine + imag * sine).astype(jnp.bfloat16)
                shift_im = (imag * cosine - real * sine).astype(jnp.bfloat16)
                scores += lax.dot_general(shift_re.reshape(trans * TILE, PIECE), views(cols), contract_last,
                                          preferred_element_type=jnp.float32)
                scores += lax.dot_general(shift_im.reshape(trans * TILE, PIECE), views(icols), contract_last,
                                          preferred_element_type=jnp.float32)
            full = scores.reshape(trans, TILE, ori) + pens[mine, :][None]
            highest = jnp.max(jnp.max(full, axis=0), axis=1, keepdims=True)
            total = jnp.zeros((TILE, ori), jnp.float32)
            moment_x = jnp.zeros((TILE, ori), jnp.float32)
            moment_y = jnp.zeros((TILE, ori), jnp.float32)
            for t in range(trans):
                term = jnp.exp(full[t] - highest)
                total += term
                moment_x += term * here[:, trans + 1 + t:trans + 2 + t]
                moment_y += term * here[:, 2 * trans + 1 + t:2 * trans + 2 + t]
            total = jnp.sum(total, axis=1, keepdims=True)
            moment_x = jnp.sum(moment_x, axis=1, keepdims=True)
            moment_y = jnp.sum(moment_y, axis=1, keepdims=True)
            lanes = lax.broadcasted_iota(jnp.int32, (TILE, 128), 1)
            stats[mine, :] = jnp.where(
                lanes == 0, highest,
                jnp.where(lanes == 1, total, jnp.where(lanes == 2, moment_x,
                                                       jnp.where(lanes == 3, moment_y, 0.0))))

        back = sum(
            lax.dot_general(part, pick, (((0,), (0,)), ((), ())), preferred_element_type=jnp.float32)
            for part in three(stats[...])
        )
        out_ref[place] = back[:8, :]


def class_stats(jobs, ids, label, table, wtab, dtab, penalty, x_parts, q_parts, trans, slots, features):
    rows_all = sum(part.shape[0] - 8 for part in x_parts)
    rows_q, width = q_parts[0].shape[1:]
    ori = rows_q * len(q_parts)
    extra = [] if penalty is None else [penalty]
    vmem = pl.BlockSpec(memory_space=pltpu.VMEM)
    return pl.pallas_call(
        functools.partial(stats_kernel, trans, jobs, len(q_parts), len(x_parts), penalty is not None),
        out_shape=jax.ShapeDtypeStruct((len(jobs), 8, rows_all), jnp.float32),
        in_specs=[pl.BlockSpec(memory_space=pltpu.SMEM)]
        + [vmem] * (4 + len(extra) + len(x_parts) + len(q_parts)),
        out_specs=vmem,
        scratch_shapes=[
            pltpu.VMEM((slots, width), jnp.float32),
            pltpu.VMEM((slots, ori), jnp.float32),
            pltpu.VMEM((slots, features), jnp.float32),
            pltpu.VMEM((slots, 128), jnp.float32),
        ],
        compiler_params=pltpu.CompilerParams(vmem_limit_bytes=28 * 1024 * 1024),
        cost_estimate=pl.CostEstimate(
            flops=20 * len(jobs) * slots * trans * width * (ori + 256),
            bytes_accessed=(rows_all + ori) * width * 2,
            transcendentals=0,
        ),
    )(ids, label, table, wtab, dtab, *extra, *x_parts, *q_parts)


def on_device(particles, candidates, ctf_ids, offsets, ctf_table, sigma_sq, projections):
    pose_count = lax.axis_size("pose")
    dom_count = lax.axis_size("dom")
    pose = lax.axis_index("pose")
    local = projections.shape[0]
    class_total = local * pose_count
    rows, picks = candidates.shape
    trans = offsets.shape[2]
    pixels = sigma_sq.shape[0]
    capacity = 3 * rows * picks // class_total
    share = min(SHARE, pose_count)
    share_bits = [1 << b for b in range(share.bit_length() - 1)]
    families = pose_count // share

    def slots_for(blocks):
        return -(-min(blocks * capacity, blocks * rows) // TILE) * TILE

    dom_bits = [1 << b for b in range(dom_count.bit_length() - 1)][::-1]

    order = [0]
    for bit in share_bits[::-1]:
        order = order + [member ^ bit for member in order]

    near = len([member for member in order if bin(member).count("1") < 2])

    offset_t = offsets.transpose(1, 2, 0).astype(jnp.float32)
    combo = (offset_t[0] + REACH) * (2 * REACH + 1) + (offset_t[1] + REACH)
    meta = jnp.concatenate(
        [combo, ctf_ids[None, :].astype(jnp.float32), offset_t[0], offset_t[1],
         candidates.T.astype(jnp.float32)], axis=0)
    features = -(-meta.shape[0] // 16) * 16
    meta = jnp.pad(meta, ((0, features - meta.shape[0]), (0, 0)), constant_values=-1.0)
    meta = meta.reshape(features // 8, 8, rows).transpose(1, 0, 2).reshape(8, -1).astype(jnp.bfloat16)
    meta = jnp.pad(meta, ((0, 0), (0, particles.shape[1] - meta.shape[1])))
    block = jnp.concatenate([particles, meta], axis=0)

    single = {bit: swap(block, "pose", bit) for bit in share_bits[::-1]}
    own_pieces = [projections] + [swap(projections, "dom", bit) for bit in dom_bits]
    own_pieces = own_pieces + [swap(own_pieces[1], "dom", bit) for bit in dom_bits[1:]]
    chunks = [projections[spot:spot + 1] for spot in range(local)]
    far = [[swap(chunks[0], "pose", family * share)] for family in range(1, families)]
    weight = ctf_table / sigma_sq[None, :]
    wtab = jnp.concatenate(split_three(weight), axis=0)
    dtab = jnp.concatenate(split_three(weight * ctf_table), axis=0)
    own_penalty = own_penalties(dtab, own_pieces)

    owner = pose ^ (jnp.arange(families, dtype=jnp.int32) * share)
    ids = (owner[:, None] * local + jnp.arange(local, dtype=jnp.int32)[None, :]).reshape(-1)
    single, chunks, far, own_penalty, ids = lax.optimization_barrier(
        (single, chunks, far, own_penalty, ids))

    x_parts = []
    for member in order:
        bits = [bit for bit in share_bits if member & bit]
        part = single[bits[-1]] if bits else block
        for bit in bits[:-1]:
            part = swap(part, "pose", bit)
        x_parts.append(part)
    for family in range(1, families):
        far[family - 1] += [swap(chunk, "pose", family * share) for chunk in chunks[1:]]
    table, label = phase_table(pixels)
    table, label = jnp.asarray(table), jnp.asarray(label)
    results = {}
    latest = []

    def run(key, jobs, members, penalty, first, last):
        turn = ids
        if latest:
            turn, results[latest[-1]] = lax.optimization_barrier((turn, results[latest[-1]]))
        results[key] = class_stats(jobs, turn, label, table, wtab, dtab, penalty, x_parts[first:last],
                                   members, trans, slots_for(last - first), features)
        latest.append(key)

    own_jobs = [(spot, spot) for spot in range(local)]
    run("near", own_jobs, own_pieces, own_penalty, 0, near)
    for family in range(1, families):
        for spot in range(local):
            pieces = [far[family - 1][spot]]
            for hop, bit in enumerate(dom_bits):
                if spot or hop:
                    key = "last" if hop and spot else "near"
                    pieces[hop:], results[key] = lax.optimization_barrier((pieces[hop:], results[key]))
                pieces = pieces + [swap(member, "dom", bit) for member in pieces]
            index = family * local + spot
            run(index, [(index, 0)], pieces, None, 0, share)
            if "last" not in results:
                run("last", own_jobs, own_pieces, own_penalty, near, share)

    results = dict(zip(results, lax.optimization_barrier(tuple(results.values()))))
    own = []
    for place, member in enumerate(order):
        block = []
        for spot in range(families * local):
            key, at = spot, 0
            if spot < local:
                key, at = ("near" if place < near else "last"), spot
            start = (place - (near if key == "last" else 0)) * rows
            block.append(results[key][at:at + 1, :4, start:start + rows])
        block = jnp.concatenate(block, axis=0)
        block = swap(block, "pose", member) if member else block
        own += [(member, spot, block[spot]) for spot in range(families * local)]

    cand = candidates.T
    owner = cand // local
    beyond = (owner ^ pose) // share
    within = (owner ^ pose) % share
    position = beyond * local + cand % local
    picked = jnp.zeros((picks, 4, rows), jnp.float32)
    for member, spot, block in own:
        hit = (within == member) & (position == spot)
        picked = jnp.where(hit[:, None, :], block[None], picked)
    log_weight = picked[:, 0] + jnp.log(picked[:, 1])
    raw_weight = jnp.exp(log_weight - jnp.max(log_weight, axis=0, keepdims=True))
    class_prob = raw_weight / jnp.sum(raw_weight, axis=0, keepdims=True)
    mean_x = jnp.sum(class_prob * picked[:, 2] / picked[:, 1], axis=0)
    mean_y = jnp.sum(class_prob * picked[:, 3] / picked[:, 1], axis=0)
    return (class_prob.T, jnp.stack([mean_x, mean_y], axis=1))


def solution(mesh):
    in_specs = (
        P(("pose", "dom"), None),
        P(("pose", "dom"), None),
        P(("pose", "dom")),
        P(("pose", "dom"), None, None),
        P(),
        P(),
        P("pose", "dom", None),
    )
    out_specs = (P(("pose", "dom"), None), P(("pose", "dom"), None))
    return jax.shard_map(
        on_device, mesh=mesh, in_specs=in_specs, out_specs=out_specs, check_vma=False
    )
```

```python
import functools

import jax
import jax.numpy as jnp
import ml_dtypes
import numpy as np
from jax import lax
from jax.experimental import pallas as pl
from jax.experimental.pallas import tpu as pltpu
from jax.sharding import PartitionSpec as P

BOX = 128
GRID_X = 64
REACH = 3
SHARE = 4
TILE = 32
HALF = 16
CHUNK = 512
PIECE = 256
HIGHEST = lax.Precision.HIGHEST


def split_three(values):
    parts = []
    for _ in range(3):
        part = lax.reduce_precision(values, 8, 7)
        parts.append(part.astype(jnp.bfloat16))
        values = values - part
    return parts


def phase_table(pixel_count):
    levels = np.arange(-REACH, REACH + 1)
    pixel = np.arange(pixel_count)
    shift_x = np.repeat(levels, levels.size)[:, None]
    shift_y = np.tile(levels, levels.size)[:, None]
    angle = 2.0 * np.pi / BOX * (shift_x * (pixel % GRID_X - 32) + shift_y * (pixel // GRID_X))
    rest = np.concatenate([np.cos(angle), np.sin(angle)], axis=1).astype(np.float32)
    parts = []
    for _ in range(3):
        part = rest.astype(ml_dtypes.bfloat16)
        parts.append(part)
        rest = rest - part.astype(np.float32)
    rows = np.concatenate(parts, axis=0)
    count = levels.size**2
    padded = np.zeros((256, 2 * pixel_count), ml_dtypes.bfloat16)
    padded[: rows.shape[0]] = rows
    label = np.full((1, 256), -1.0, np.float32)
    label[0, : rows.shape[0]] = np.arange(rows.shape[0]) % count
    return (padded, label)


def swap(values, axis, bit):
    count = lax.axis_size(axis)
    return lax.ppermute(values, axis, [(index, index ^ bit) for index in range(count)])


def three(values):
    high = values.astype(jnp.bfloat16)
    rest = values - high.astype(jnp.float32)
    middle = rest.astype(jnp.bfloat16)
    return [high, middle, (rest - middle.astype(jnp.float32)).astype(jnp.bfloat16)]


contract_last = (((1,), (1,)), ((), ()))


def penalties_of(views, dtab_ref, ori, pixels):
    groups = dtab_ref.shape[0] // 3
    parted = jnp.zeros((3 * groups, ori), jnp.float32)
    for first in range(0, pixels, CHUNK):
        real = views(slice(first, first + CHUNK)).astype(jnp.float32)
        imag = views(slice(pixels + first, pixels + first + CHUNK)).astype(jnp.float32)
        for part in three(real * real + imag * imag)[:2]:
            parted += lax.dot_general(dtab_ref[:, first:first + CHUNK], part, contract_last,
                                      preferred_element_type=jnp.float32)
    return -0.5 * (parted[:groups] + parted[groups:2 * groups] + parted[2 * groups:])


def views_of(q_refs, spots):
    def views(cols):
        return jnp.concatenate([member[spot, :, cols] for member, spot in zip(q_refs, spots)], axis=0)
    return views


def penalty_kernel(pieces, dtab_ref, *refs):
    out_ref = refs[pieces]
    for place in range(out_ref.shape[0]):
        views = views_of(refs[:pieces], [place] * pieces)
        out_ref[place] = penalties_of(views, dtab_ref, out_ref.shape[2], dtab_ref.shape[1])


def own_penalties(dtab, pieces):
    classes, rows_q, width = pieces[0].shape
    ori = rows_q * len(pieces)
    vmem = pl.BlockSpec(memory_space=pltpu.VMEM)
    return pl.pallas_call(
        functools.partial(penalty_kernel, len(pieces)),
        out_shape=jax.ShapeDtypeStruct((classes, dtab.shape[0] // 3, ori), jnp.float32),
        in_specs=[vmem] * (1 + len(pieces)),
        out_specs=vmem,
        compiler_params=pltpu.CompilerParams(vmem_limit_bytes=24 * 1024 * 1024),
    )(dtab, *pieces)


def stats_kernel(trans, jobs, pieces, share, size, have_penalty, ids_ref, label_ref, table_ref, wtab_ref,
                 dtab_ref, *refs):
    if have_penalty:
        penalty_ref, refs = refs[0], refs[1:]
    x_refs, refs = refs[:share], refs[share:]
    q_refs = refs[:pieces]
    out_ref, uv, pens, info, stats = refs[pieces:]
    rows_all = out_ref.shape[2]
    rows = rows_all // share
    features = info.shape[1]
    slots = uv.shape[0]
    pixels = uv.shape[1] // 2
    ori = pens.shape[1]
    groups = dtab_ref.shape[0] // 3

    def particles(cols):
        return jnp.concatenate([member[:rows, cols] for member in x_refs], axis=0)

    below = [member[rows:rows + 8, :features // 8 * rows].astype(jnp.float32) for member in x_refs]
    meta = jnp.concatenate(
        [jnp.concatenate([block[:, at * rows:(at + 1) * rows] for at in range(features // 8)], axis=0)
         for block in below], axis=1)
    named = meta[3 * trans + 1:, :]
    meta = meta.astype(jnp.bfloat16)
    before = lax.broadcasted_iota(jnp.int32, (rows_all, rows_all), 0)
    after = lax.broadcasted_iota(jnp.int32, (rows_all, rows_all), 1)
    upper = jnp.where(before <= after, 1.0, 0.0).astype(jnp.bfloat16)
    label = label_ref[...]

    for place, (index, spot) in enumerate(jobs):
        views = views_of(q_refs, [spot] * pieces)
        wanted = ids_ref[index].astype(jnp.float32)
        names = jnp.max(jnp.where(named == wanted, 1.0, 0.0), axis=0, keepdims=True)
        ahead = jnp.dot(jnp.broadcast_to(names, (16, rows_all)).astype(jnp.bfloat16), upper,
                        preferred_element_type=jnp.float32)[:1]
        rank = jnp.where(names > 0.0, ahead - 1.0, -1.0).astype(jnp.int32)
        tiles = (jnp.max(ahead).astype(jnp.int32) + (size - 1)) // size

        row = lax.broadcasted_iota(jnp.int32, (slots, rows_all), 0)
        pick = jnp.where(rank == row, 1.0, 0.0).astype(jnp.bfloat16)
        info[...] = lax.dot_general(pick, meta, contract_last, preferred_element_type=jnp.float32)
        lane = lax.broadcasted_iota(jnp.int32, (slots, 3 * groups), 1)
        group_hot = jnp.where(info[:, trans:trans + 1] == (lane % groups).astype(jnp.float32), 1.0, 0.0)
        group_hot = group_hot.astype(jnp.bfloat16)
        stats[...] = jnp.zeros_like(stats)
        for first in range(0, pixels, CHUNK):
            weight = jnp.dot(group_hot, wtab_ref[:, first:first + CHUNK], preferred_element_type=jnp.float32)
            for start in (first, pixels + first):
                span = slice(start, start + CHUNK)
                uv[:, span] = weight * jnp.dot(pick, particles(span), preferred_element_type=jnp.float32)
        penalty = penalty_ref[spot] if have_penalty else penalties_of(views, dtab_ref, ori, pixels)
        pens[...] = jnp.dot(group_hot, jnp.concatenate(three(penalty), axis=0),
                            preferred_element_type=jnp.float32)

        @pl.loop(0, tiles)
        def _(tile):
            mine = pl.ds(pl.multiple_of(tile * size, size), size)
            here = info[mine, :]
            hot = jnp.concatenate(
                [jnp.where(here[:, t:t + 1] == label, 1.0, 0.0) for t in range(trans)], axis=0
            ).astype(jnp.bfloat16)
            scores = jnp.zeros((trans * size, ori), jnp.float32)
            for first in range(0, pixels, PIECE):
                cols = slice(first, first + PIECE)
                icols = slice(pixels + first, pixels + first + PIECE)
                cosine = jnp.dot(hot, table_ref[:, cols], preferred_element_type=jnp.float32)
                sine = jnp.dot(hot, table_ref[:, icols], preferred_element_type=jnp.float32)
                cosine = cosine.reshape(trans, size, PIECE)
                sine = sine.reshape(trans, size, PIECE)
                real = uv[mine, cols][None]
                imag = uv[mine, icols][None]
                shift_re = (real * cosine + imag * sine).astype(jnp.bfloat16)
                shift_im = (imag * cosine - real * sine).astype(jnp.bfloat16)
                scores += lax.dot_general(shift_re.reshape(trans * size, PIECE), views(cols), contract_last,
                                          preferred_element_type=jnp.float32)
                scores += lax.dot_general(shift_im.reshape(trans * size, PIECE), views(icols), contract_last,
                                          preferred_element_type=jnp.float32)
            full = scores.reshape(trans, size, ori) + pens[mine, :][None]
            highest = jnp.max(jnp.max(full, axis=0), axis=1, keepdims=True)
            total = jnp.zeros((size, ori), jnp.float32)
            moment_x = jnp.zeros((size, ori), jnp.float32)
            moment_y = jnp.zeros((size, ori), jnp.float32)
            for t in range(trans):
                term = jnp.exp(full[t] - highest)
                total += term
                moment_x += term * here[:, trans + 1 + t:trans + 2 + t]
                moment_y += term * here[:, 2 * trans + 1 + t:2 * trans + 2 + t]
            total = jnp.sum(total, axis=1, keepdims=True)
            moment_x = jnp.sum(moment_x, axis=1, keepdims=True)
            moment_y = jnp.sum(moment_y, axis=1, keepdims=True)
            lanes = lax.broadcasted_iota(jnp.int32, (size, 128), 1)
            stats[mine, :] = jnp.where(
                lanes == 0, highest,
                jnp.where(lanes == 1, total, jnp.where(lanes == 2, moment_x,
                                                       jnp.where(lanes == 3, moment_y, 0.0))))

        back = sum(
            lax.dot_general(part, pick, (((0,), (0,)), ((), ())), preferred_element_type=jnp.float32)
            for part in three(stats[...])
        )
        out_ref[place] = back[:8, :]


def class_stats(jobs, ids, label, table, wtab, dtab, penalty, x_parts, q_parts, trans, slots, features):
    rows_all = sum(part.shape[0] - 8 for part in x_parts)
    rows_q, width = q_parts[0].shape[1:]
    ori = rows_q * len(q_parts)
    extra = [] if penalty is None else [penalty]
    vmem = pl.BlockSpec(memory_space=pltpu.VMEM)
    return pl.pallas_call(
        functools.partial(stats_kernel, trans, jobs, len(q_parts), len(x_parts), HALF if len(x_parts) == 1 else TILE,
                          penalty is not None),
        out_shape=jax.ShapeDtypeStruct((len(jobs), 8, rows_all), jnp.float32),
        in_specs=[pl.BlockSpec(memory_space=pltpu.SMEM)]
        + [vmem] * (4 + len(extra) + len(x_parts) + len(q_parts)),
        out_specs=vmem,
        scratch_shapes=[
            pltpu.VMEM((slots, width), jnp.float32),
            pltpu.VMEM((slots, ori), jnp.float32),
            pltpu.VMEM((slots, features), jnp.float32),
            pltpu.VMEM((slots, 128), jnp.float32),
        ],
        compiler_params=pltpu.CompilerParams(vmem_limit_bytes=20 * 1024 * 1024),
        cost_estimate=pl.CostEstimate(
            flops=20 * len(jobs) * slots * trans * width * (ori + 256),
            bytes_accessed=(rows_all + ori) * width * 2,
            transcendentals=0,
        ),
    )(ids, label, table, wtab, dtab, *extra, *x_parts, *q_parts)


def on_device(particles, candidates, ctf_ids, offsets, ctf_table, sigma_sq, projections):
    pose_count = lax.axis_size("pose")
    dom_count = lax.axis_size("dom")
    pose = lax.axis_index("pose")
    local = projections.shape[0]
    class_total = local * pose_count
    rows, picks = candidates.shape
    trans = offsets.shape[2]
    pixels = sigma_sq.shape[0]
    capacity = 3 * rows * picks // class_total
    share = min(SHARE, pose_count)
    share_bits = [1 << b for b in range(share.bit_length() - 1)]
    families = pose_count // share

    def slots_for(blocks):
        return -(-min(blocks * capacity, blocks * rows) // TILE) * TILE

    dom_bits = [1 << b for b in range(dom_count.bit_length() - 1)][::-1]

    order = [0]
    for bit in share_bits[::-1]:
        order = order + [member ^ bit for member in order]

    near = len([member for member in order if bin(member).count("1") < 2])

    offset_t = offsets.transpose(1, 2, 0).astype(jnp.float32)
    combo = (offset_t[0] + REACH) * (2 * REACH + 1) + (offset_t[1] + REACH)
    meta = jnp.concatenate(
        [combo, ctf_ids[None, :].astype(jnp.float32), offset_t[0], offset_t[1],
         candidates.T.astype(jnp.float32)], axis=0)
    features = -(-meta.shape[0] // 16) * 16
    meta = jnp.pad(meta, ((0, features - meta.shape[0]), (0, 0)), constant_values=-1.0)
    meta = meta.reshape(features // 8, 8, rows).transpose(1, 0, 2).reshape(8, -1).astype(jnp.bfloat16)
    meta = jnp.pad(meta, ((0, 0), (0, particles.shape[1] - meta.shape[1])))
    block = jnp.concatenate([particles, meta], axis=0)

    single = {bit: swap(block, "pose", bit) for bit in share_bits[::-1]}
    own_pieces = [projections] + [swap(projections, "dom", bit) for bit in dom_bits]
    own_pieces = own_pieces + [swap(own_pieces[1], "dom", bit) for bit in dom_bits[1:]]
    chunks = [projections[spot:spot + 1] for spot in range(local)]
    far = [[swap(chunks[0], "pose", family * share)] for family in range(1, families)]
    weight = ctf_table / sigma_sq[None, :]
    wtab = jnp.concatenate(split_three(weight), axis=0)
    dtab = jnp.concatenate(split_three(weight * ctf_table), axis=0)
    own_penalty = own_penalties(dtab, own_pieces)

    owner = pose ^ (jnp.arange(families, dtype=jnp.int32) * share)
    ids = (owner[:, None] * local + jnp.arange(local, dtype=jnp.int32)[None, :]).reshape(-1)
    single, chunks, far, own_penalty, ids = lax.optimization_barrier(
        (single, chunks, far, own_penalty, ids))

    x_parts = []
    for member in order:
        bits = [bit for bit in share_bits if member & bit]
        part = single[bits[-1]] if bits else block
        for bit in bits[:-1]:
            part = swap(part, "pose", bit)
        x_parts.append(part)
    for family in range(1, families):
        far[family - 1] += [swap(chunk, "pose", family * share) for chunk in chunks[1:]]
    table, label = phase_table(pixels)
    table, label = jnp.asarray(table), jnp.asarray(label)
    results = {}
    latest = []

    def run(key, jobs, members, penalty, first, last):
        turn = ids
        if latest:
            turn, results[latest[-1]] = lax.optimization_barrier((turn, results[latest[-1]]))
        results[key] = class_stats(jobs, turn, label, table, wtab, dtab, penalty, x_parts[first:last],
                                   members, trans, slots_for(last - first), features)
        latest.append(key)

    own_jobs = [(spot, spot) for spot in range(local)]
    run("near", own_jobs, own_pieces, own_penalty, 0, near)
    for family in range(1, families):
        for spot in range(local):
            pieces = [far[family - 1][spot]]
            for hop, bit in enumerate(dom_bits):
                if spot or hop:
                    key = "last" if hop and spot else "near"
                    pieces[hop:], results[key] = lax.optimization_barrier((pieces[hop:], results[key]))
                pieces = pieces + [swap(member, "dom", bit) for member in pieces]
            index = family * local + spot
            run(index, [(index, 0)], pieces, None, 0, share)
            if "last" not in results:
                run("last", own_jobs, own_pieces, own_penalty, near, share)

    results = dict(zip(results, lax.optimization_barrier(tuple(results.values()))))
    own = []
    for place, member in enumerate(order):
        block = []
        for spot in range(families * local):
            key, at = spot, 0
            if spot < local:
                key, at = ("near" if place < near else "last"), spot
            start = (place - (near if key == "last" else 0)) * rows
            block.append(results[key][at:at + 1, :4, start:start + rows])
        block = jnp.concatenate(block, axis=0)
        block = swap(block, "pose", member) if member else block
        own += [(member, spot, block[spot]) for spot in range(families * local)]

    cand = candidates.T
    owner = cand // local
    beyond = (owner ^ pose) // share
    within = (owner ^ pose) % share
    position = beyond * local + cand % local
    picked = jnp.zeros((picks, 4, rows), jnp.float32)
    for member, spot, block in own:
        hit = (within == member) & (position == spot)
        picked = jnp.where(hit[:, None, :], block[None], picked)
    log_weight = picked[:, 0] + jnp.log(picked[:, 1])
    raw_weight = jnp.exp(log_weight - jnp.max(log_weight, axis=0, keepdims=True))
    class_prob = raw_weight / jnp.sum(raw_weight, axis=0, keepdims=True)
    mean_x = jnp.sum(class_prob * picked[:, 2] / picked[:, 1], axis=0)
    mean_y = jnp.sum(class_prob * picked[:, 3] / picked[:, 1], axis=0)
    return (class_prob.T, jnp.stack([mean_x, mean_y], axis=1))


def solution(mesh):
    in_specs = (
        P(("pose", "dom"), None),
        P(("pose", "dom"), None),
        P(("pose", "dom")),
        P(("pose", "dom"), None, None),
        P(),
        P(),
        P("pose", "dom", None),
    )
    out_specs = (P(("pose", "dom"), None), P(("pose", "dom"), None))
    return jax.shard_map(
        on_device, mesh=mesh, in_specs=in_specs, out_specs=out_specs, check_vma=False
    )
```

```python
import functools

import jax
import jax.numpy as jnp
import ml_dtypes
import numpy as np
from jax import lax
from jax.experimental import pallas as pl
from jax.experimental.pallas import tpu as pltpu
from jax.sharding import PartitionSpec as P

BOX = 128
GRID_X = 64
REACH = 3
SHARE = 4
TILE = 32
CHUNK = 512
PIECE = 256
HIGHEST = lax.Precision.HIGHEST


def split_three(values):
    parts = []
    for _ in range(3):
        part = lax.reduce_precision(values, 8, 7)
        parts.append(part.astype(jnp.bfloat16))
        values = values - part
    return parts


def phase_table(pixel_count):
    levels = np.arange(-REACH, REACH + 1)
    pixel = np.arange(pixel_count)
    shift_x = np.repeat(levels, levels.size)[:, None]
    shift_y = np.tile(levels, levels.size)[:, None]
    angle = 2.0 * np.pi / BOX * (shift_x * (pixel % GRID_X - 32) + shift_y * (pixel // GRID_X))
    rest = np.concatenate([np.cos(angle), np.sin(angle)], axis=1).astype(np.float32)
    parts = []
    for _ in range(3):
        part = rest.astype(ml_dtypes.bfloat16)
        parts.append(part)
        rest = rest - part.astype(np.float32)
    rows = np.concatenate(parts, axis=0)
    count = levels.size**2
    padded = np.zeros((256, 2 * pixel_count), ml_dtypes.bfloat16)
    padded[: rows.shape[0]] = rows
    label = np.full((1, 256), -1.0, np.float32)
    label[0, : rows.shape[0]] = np.arange(rows.shape[0]) % count
    return (padded, label)


def swap(values, axis, bit):
    count = lax.axis_size(axis)
    return lax.ppermute(values, axis, [(index, index ^ bit) for index in range(count)])


def three(values):
    high = values.astype(jnp.bfloat16)
    rest = values - high.astype(jnp.float32)
    middle = rest.astype(jnp.bfloat16)
    return [high, middle, (rest - middle.astype(jnp.float32)).astype(jnp.bfloat16)]


contract_last = (((1,), (1,)), ((), ()))


def penalties_of(views, dtab_ref, ori, pixels):
    groups = dtab_ref.shape[0] // 3
    parted = jnp.zeros((3 * groups, ori), jnp.float32)
    for first in range(0, pixels, CHUNK):
        real = views(slice(first, first + CHUNK)).astype(jnp.float32)
        imag = views(slice(pixels + first, pixels + first + CHUNK)).astype(jnp.float32)
        for part in three(real * real + imag * imag)[:2]:
            parted += lax.dot_general(dtab_ref[:, first:first + CHUNK], part, contract_last,
                                      preferred_element_type=jnp.float32)
    return -0.5 * (parted[:groups] + parted[groups:2 * groups] + parted[2 * groups:])


def views_of(q_refs, spots):
    def views(cols):
        return jnp.concatenate([member[spot, :, cols] for member, spot in zip(q_refs, spots)], axis=0)
    return views


def penalty_kernel(pieces, dtab_ref, *refs):
    out_ref = refs[pieces]
    for place in range(out_ref.shape[0]):
        views = views_of(refs[:pieces], [place] * pieces)
        out_ref[place] = penalties_of(views, dtab_ref, out_ref.shape[2], dtab_ref.shape[1])


def own_penalties(dtab, pieces):
    classes, rows_q, width = pieces[0].shape
    ori = rows_q * len(pieces)
    vmem = pl.BlockSpec(memory_space=pltpu.VMEM)
    return pl.pallas_call(
        functools.partial(penalty_kernel, len(pieces)),
        out_shape=jax.ShapeDtypeStruct((classes, dtab.shape[0] // 3, ori), jnp.float32),
        in_specs=[vmem] * (1 + len(pieces)),
        out_specs=vmem,
        compiler_params=pltpu.CompilerParams(vmem_limit_bytes=24 * 1024 * 1024),
    )(dtab, *pieces)


def stats_kernel(trans, jobs, pieces, share, have_penalty, ids_ref, label_ref, table_ref, wtab_ref,
                 dtab_ref, *refs):
    if have_penalty:
        penalty_ref, refs = refs[0], refs[1:]
    x_refs, refs = refs[:share], refs[share:]
    q_refs = refs[:pieces]
    out_ref, uv, pens, info, stats = refs[pieces:]
    rows_all = out_ref.shape[2]
    rows = rows_all // share
    features = info.shape[1]
    slots = uv.shape[0]
    pixels = uv.shape[1] // 2
    ori = pens.shape[1]
    groups = dtab_ref.shape[0] // 3

    def particles(cols):
        return jnp.concatenate([member[:rows, cols] for member in x_refs], axis=0)

    below = [member[rows:rows + 8, :features // 8 * rows].astype(jnp.float32) for member in x_refs]
    meta = jnp.concatenate(
        [jnp.concatenate([block[:, at * rows:(at + 1) * rows] for at in range(features // 8)], axis=0)
         for block in below], axis=1)
    named = meta[3 * trans + 1:, :]
    meta = meta.astype(jnp.bfloat16)
    before = lax.broadcasted_iota(jnp.int32, (rows_all, rows_all), 0)
    after = lax.broadcasted_iota(jnp.int32, (rows_all, rows_all), 1)
    upper = jnp.where(before <= after, 1.0, 0.0).astype(jnp.bfloat16)
    label = label_ref[...]

    for place, (index, spot) in enumerate(jobs):
        views = views_of(q_refs, [spot] * pieces)
        wanted = ids_ref[index].astype(jnp.float32)
        names = jnp.max(jnp.where(named == wanted, 1.0, 0.0), axis=0, keepdims=True)
        ahead = jnp.dot(jnp.broadcast_to(names, (16, rows_all)).astype(jnp.bfloat16), upper,
                        preferred_element_type=jnp.float32)[:1]
        rank = jnp.where(names > 0.0, ahead - 1.0, -1.0).astype(jnp.int32)
        tiles = (jnp.max(ahead).astype(jnp.int32) + (TILE - 1)) // TILE

        row = lax.broadcasted_iota(jnp.int32, (slots, rows_all), 0)
        pick = jnp.where(rank == row, 1.0, 0.0).astype(jnp.bfloat16)
        info[...] = lax.dot_general(pick, meta, contract_last, preferred_element_type=jnp.float32)
        lane = lax.broadcasted_iota(jnp.int32, (slots, 3 * groups), 1)
        group_hot = jnp.where(info[:, trans:trans + 1] == (lane % groups).astype(jnp.float32), 1.0, 0.0)
        group_hot = group_hot.astype(jnp.bfloat16)
        stats[...] = jnp.zeros_like(stats)
        for first in range(0, pixels, CHUNK):
            weight = jnp.dot(group_hot, wtab_ref[:, first:first + CHUNK], preferred_element_type=jnp.float32)
            for start in (first, pixels + first):
                span = slice(start, start + CHUNK)
                uv[:, span] = weight * jnp.dot(pick, particles(span), preferred_element_type=jnp.float32)
        penalty = penalty_ref[spot] if have_penalty else penalties_of(views, dtab_ref, ori, pixels)
        pens[...] = jnp.dot(group_hot, jnp.concatenate(three(penalty), axis=0),
                            preferred_element_type=jnp.float32)

        def one_tile(start, size):
            mine = pl.ds(pl.multiple_of(start, TILE), size)
            here = info[mine, :]
            hot = jnp.concatenate(
                [jnp.where(here[:, t:t + 1] == label, 1.0, 0.0) for t in range(trans)], axis=0
            ).astype(jnp.bfloat16)
            scores = jnp.zeros((trans * size, ori), jnp.float32)
            for first in range(0, pixels, PIECE):
                cols = slice(first, first + PIECE)
                icols = slice(pixels + first, pixels + first + PIECE)
                cosine = jnp.dot(hot, table_ref[:, cols], preferred_element_type=jnp.float32)
                sine = jnp.dot(hot, table_ref[:, icols], preferred_element_type=jnp.float32)
                cosine = cosine.reshape(trans, size, PIECE)
                sine = sine.reshape(trans, size, PIECE)
                real = uv[mine, cols][None]
                imag = uv[mine, icols][None]
                shift_re = (real * cosine + imag * sine).astype(jnp.bfloat16)
                shift_im = (imag * cosine - real * sine).astype(jnp.bfloat16)
                scores += lax.dot_general(shift_re.reshape(trans * size, PIECE), views(cols), contract_last,
                                          preferred_element_type=jnp.float32)
                scores += lax.dot_general(shift_im.reshape(trans * size, PIECE), views(icols), contract_last,
                                          preferred_element_type=jnp.float32)
            full = scores.reshape(trans, size, ori) + pens[mine, :][None]
            highest = jnp.max(jnp.max(full, axis=0), axis=1, keepdims=True)
            total = jnp.zeros((size, ori), jnp.float32)
            moment_x = jnp.zeros((size, ori), jnp.float32)
            moment_y = jnp.zeros((size, ori), jnp.float32)
            for t in range(trans):
                term = jnp.exp(full[t] - highest)
                total += term
                moment_x += term * here[:, trans + 1 + t:trans + 2 + t]
                moment_y += term * here[:, 2 * trans + 1 + t:2 * trans + 2 + t]
            total = jnp.sum(total, axis=1, keepdims=True)
            moment_x = jnp.sum(moment_x, axis=1, keepdims=True)
            moment_y = jnp.sum(moment_y, axis=1, keepdims=True)
            lanes = lax.broadcasted_iota(jnp.int32, (size, 128), 1)
            stats[mine, :] = jnp.where(
                lanes == 0, highest,
                jnp.where(lanes == 1, total, jnp.where(lanes == 2, moment_x,
                                                       jnp.where(lanes == 3, moment_y, 0.0))))

        if share > 1 and slots >= 2 * TILE:
            @pl.loop(0, tiles // 2)
            def _(pair):
                one_tile(pair * (2 * TILE), 2 * TILE)

            @pl.when(tiles % 2 == 1)
            def _():
                one_tile((tiles - 1) * TILE, TILE)
        else:
            @pl.loop(0, tiles)
            def _(tile):
                one_tile(tile * TILE, TILE)

        back = sum(
            lax.dot_general(part, pick, (((0,), (0,)), ((), ())), preferred_element_type=jnp.float32)
            for part in three(stats[...])
        )
        out_ref[place] = back[:8, :]


def class_stats(jobs, ids, label, table, wtab, dtab, penalty, x_parts, q_parts, trans, slots, features):
    rows_all = sum(part.shape[0] - 8 for part in x_parts)
    rows_q, width = q_parts[0].shape[1:]
    ori = rows_q * len(q_parts)
    extra = [] if penalty is None else [penalty]
    vmem = pl.BlockSpec(memory_space=pltpu.VMEM)
    return pl.pallas_call(
        functools.partial(stats_kernel, trans, jobs, len(q_parts), len(x_parts), penalty is not None),
        out_shape=jax.ShapeDtypeStruct((len(jobs), 8, rows_all), jnp.float32),
        in_specs=[pl.BlockSpec(memory_space=pltpu.SMEM)]
        + [vmem] * (4 + len(extra) + len(x_parts) + len(q_parts)),
        out_specs=vmem,
        scratch_shapes=[
            pltpu.VMEM((slots, width), jnp.float32),
            pltpu.VMEM((slots, ori), jnp.float32),
            pltpu.VMEM((slots, features), jnp.float32),
            pltpu.VMEM((slots, 128), jnp.float32),
        ],
        compiler_params=pltpu.CompilerParams(vmem_limit_bytes=28 * 1024 * 1024),
        cost_estimate=pl.CostEstimate(
            flops=20 * len(jobs) * slots * trans * width * (ori + 256),
            bytes_accessed=(rows_all + ori) * width * 2,
            transcendentals=0,
        ),
    )(ids, label, table, wtab, dtab, *extra, *x_parts, *q_parts)


def on_device(particles, candidates, ctf_ids, offsets, ctf_table, sigma_sq, projections):
    pose_count = lax.axis_size("pose")
    dom_count = lax.axis_size("dom")
    pose = lax.axis_index("pose")
    local = projections.shape[0]
    class_total = local * pose_count
    rows, picks = candidates.shape
    trans = offsets.shape[2]
    pixels = sigma_sq.shape[0]
    capacity = 3 * rows * picks // class_total
    share = min(SHARE, pose_count)
    share_bits = [1 << b for b in range(share.bit_length() - 1)]
    families = pose_count // share

    def slots_for(blocks):
        return -(-min(blocks * capacity, blocks * rows) // TILE) * TILE

    dom_bits = [1 << b for b in range(dom_count.bit_length() - 1)][::-1]

    order = [0]
    for bit in share_bits[::-1]:
        order = order + [member ^ bit for member in order]

    near = len([member for member in order if bin(member).count("1") < 2])

    offset_t = offsets.transpose(1, 2, 0).astype(jnp.float32)
    combo = (offset_t[0] + REACH) * (2 * REACH + 1) + (offset_t[1] + REACH)
    meta = jnp.concatenate(
        [combo, ctf_ids[None, :].astype(jnp.float32), offset_t[0], offset_t[1],
         candidates.T.astype(jnp.float32)], axis=0)
    features = -(-meta.shape[0] // 16) * 16
    meta = jnp.pad(meta, ((0, features - meta.shape[0]), (0, 0)), constant_values=-1.0)
    meta = meta.reshape(features // 8, 8, rows).transpose(1, 0, 2).reshape(8, -1).astype(jnp.bfloat16)
    meta = jnp.pad(meta, ((0, 0), (0, particles.shape[1] - meta.shape[1])))
    block = jnp.concatenate([particles, meta], axis=0)

    single = {bit: swap(block, "pose", bit) for bit in share_bits[::-1]}
    own_pieces = [projections] + [swap(projections, "dom", bit) for bit in dom_bits]
    own_pieces = own_pieces + [swap(own_pieces[1], "dom", bit) for bit in dom_bits[1:]]
    chunks = [projections[spot:spot + 1] for spot in range(local)]
    far = [[swap(chunks[0], "pose", family * share)] for family in range(1, families)]
    weight = ctf_table / sigma_sq[None, :]
    wtab = jnp.concatenate(split_three(weight), axis=0)
    dtab = jnp.concatenate(split_three(weight * ctf_table), axis=0)
    own_penalty = own_penalties(dtab, own_pieces)

    owner = pose ^ (jnp.arange(families, dtype=jnp.int32) * share)
    ids = (owner[:, None] * local + jnp.arange(local, dtype=jnp.int32)[None, :]).reshape(-1)
    single, chunks, far, own_penalty, ids = lax.optimization_barrier(
        (single, chunks, far, own_penalty, ids))

    x_parts = []
    for member in order:
        bits = [bit for bit in share_bits if member & bit]
        part = single[bits[-1]] if bits else block
        for bit in bits[:-1]:
            part = swap(part, "pose", bit)
        x_parts.append(part)
    for family in range(1, families):
        far[family - 1] += [swap(chunk, "pose", family * share) for chunk in chunks[1:]]
    table, label = phase_table(pixels)
    table, label = jnp.asarray(table), jnp.asarray(label)
    results = {}
    latest = []

    def run(key, jobs, members, penalty, first, last):
        turn = ids
        if latest:
            turn, results[latest[-1]] = lax.optimization_barrier((turn, results[latest[-1]]))
        results[key] = class_stats(jobs, turn, label, table, wtab, dtab, penalty, x_parts[first:last],
                                   members, trans, slots_for(last - first), features)
        latest.append(key)

    own_jobs = [(spot, spot) for spot in range(local)]
    run("near", own_jobs, own_pieces, own_penalty, 0, near)
    for family in range(1, families):
        for spot in range(local):
            pieces = [far[family - 1][spot]]
            for hop, bit in enumerate(dom_bits):
                if spot or hop:
                    key = "last" if hop and spot else "near"
                    pieces[hop:], results[key] = lax.optimization_barrier((pieces[hop:], results[key]))
                pieces = pieces + [swap(member, "dom", bit) for member in pieces]
            index = family * local + spot
            run(index, [(index, 0)], pieces, None, 0, share)
            if "last" not in results:
                run("last", own_jobs, own_pieces, own_penalty, near, share)

    results = dict(zip(results, lax.optimization_barrier(tuple(results.values()))))
    own = []
    for place, member in enumerate(order):
        block = []
        for spot in range(families * local):
            key, at = spot, 0
            if spot < local:
                key, at = ("near" if place < near else "last"), spot
            start = (place - (near if key == "last" else 0)) * rows
            block.append(results[key][at:at + 1, :4, start:start + rows])
        block = jnp.concatenate(block, axis=0)
        block = swap(block, "pose", member) if member else block
        own += [(member, spot, block[spot]) for spot in range(families * local)]

    cand = candidates.T
    owner = cand // local
    beyond = (owner ^ pose) // share
    within = (owner ^ pose) % share
    position = beyond * local + cand % local
    picked = jnp.zeros((picks, 4, rows), jnp.float32)
    for member, spot, block in own:
        hit = (within == member) & (position == spot)
        picked = jnp.where(hit[:, None, :], block[None], picked)
    log_weight = picked[:, 0] + jnp.log(picked[:, 1])
    raw_weight = jnp.exp(log_weight - jnp.max(log_weight, axis=0, keepdims=True))
    class_prob = raw_weight / jnp.sum(raw_weight, axis=0, keepdims=True)
    mean_x = jnp.sum(class_prob * picked[:, 2] / picked[:, 1], axis=0)
    mean_y = jnp.sum(class_prob * picked[:, 3] / picked[:, 1], axis=0)
    return (class_prob.T, jnp.stack([mean_x, mean_y], axis=1))


def solution(mesh):
    in_specs = (
        P(("pose", "dom"), None),
        P(("pose", "dom"), None),
        P(("pose", "dom")),
        P(("pose", "dom"), None, None),
        P(),
        P(),
        P("pose", "dom", None),
    )
    out_specs = (P(("pose", "dom"), None), P(("pose", "dom"), None))
    return jax.shard_map(
        on_device, mesh=mesh, in_specs=in_specs, out_specs=out_specs, check_vma=False
    )
```
